512 devices in a mesh: freq: 16 (over y, x_lo, core), slab: 32 (over x_hi, z).
Axes of the slice: x: 4 (x_hi: 2, x_lo: 2; x = x_hi * 2 + x_lo), y: 4, z: 16, core: 2. Of those that a mesh axis runs over, the one named last changes fastest.
Arguments:
- forward_field: bfloat16 [16, 2, 12, 1310720], P('freq', None, None, 'slab'), may hold values from -6 to 6
- adjoint_field: bfloat16 [16, 2, 12, 1310720], P('freq', None, None, 'slab'), may hold values from -6 to 6
- mass_block: float32 [3, 4, 4], replicated, may hold values from -0.075 to 0.5
- cell_size: float32 [1310720], P('slab'), may hold values from 0.3 to 3
- freq_weight: float32 [64], replicated, may hold values from 0.05 to 0.2
- freq_ids: int32 [16], P('freq'), may hold values from 0 to 63, as said below
- receiver_cells: int32 [1024], replicated, may hold values from 0 to 1310719
- step_pairs: float32 [16, 3, 1310720], P(None, None, ('slab', 'freq'))
- grad_pairs: float32 [16, 3, 1310720], P(None, None, ('slab', 'freq')), as said below
Outputs:
- gradient: float32 [3, 1310720], P(None, ('slab', 'freq'))
- direction: float32 [3, 1310720], P(None, ('slab', 'freq'))
- predicted: float32 [16], replicated
The draws below stay inside these ranges and needn't reach their ends.
Inputs may be any that keep to these rules, and one draw needn't show every extreme that they name: `freq_ids`: the slots hold distinct frequencies. `grad_pairs`: each gradient change has a positive inner product with its step.
All inputs are finite; a program needn't handle non-finite values.
Results may differ from the reference program's by a relative error of at most 0.0003.
Values sent between devices are 32-bit elements; how exact they have to be, the bound alone decides.
No kernel may reach another device: no remote copies, remote signals or barrier semaphores. Data moves between devices by JAX's collectives and lax.ppermute only.
A program may use at most 128 MiB of HBM per device.

```python
import math
import jax
import jax.numpy as jnp
from jax import lax

PAIRS = 16
NUM_FREQ = 64
RECEIVERS = 1024
FREQS = 16
CELLS_ALL = 1310720
PARAMS = 3932160


def cell_scale(key):
    key_size = jax.random.fold_in(key, 201)
    return jnp.exp(jax.random.uniform(key_size, (CELLS_ALL,), jnp.float32, jnp.log(0.3), jnp.log(3.0)))


def edge_parts(key):
    key_fwd = jax.random.fold_in(key, 301)
    key_other = jax.random.fold_in(key, 302)
    shape = (FREQS, 2, 12, CELLS_ALL)
    forward = jax.random.truncated_normal(key_fwd, -6.0, 6.0, shape, jnp.float32)
    other = jax.random.truncated_normal(key_other, -6.0, 6.0, shape, jnp.float32)
    sign = jnp.array([1.0, -1.0], dtype=jnp.float32)[None, :, None, None]
    adjoint = jnp.clip(0.5 * sign * forward + 0.85 * other, -6.0, 6.0)
    return (forward, adjoint)


def draw_forward_field(key, part):
    forward, adjoint = edge_parts(key)
    return forward.astype(jnp.bfloat16)


def draw_adjoint_field(key, part):
    forward, adjoint = edge_parts(key)
    return adjoint.astype(jnp.bfloat16)


def draw_cell_size(key, part):
    return cell_scale(key)


def draw_mass_block(key, part):
    key = jax.random.fold_in(key, 11)
    key_diag = jax.random.fold_in(key, 1)
    key_off = jax.random.fold_in(key, 2)
    diag_part = jax.random.uniform(key_diag, (3, 4), jnp.float32, 0.25, 0.5)
    raw = jax.random.uniform(key_off, (3, 4, 4), jnp.float32, -0.075, 0.075)
    unit = jnp.eye(4, dtype=jnp.float32)[None]
    off_part = 0.5 * (raw + jnp.swapaxes(raw, 1, 2)) * (1.0 - unit)
    return off_part + diag_part[:, :, None] * unit


def pair_parts(key):
    sizes = cell_scale(key)
    key_base = jax.random.fold_in(key, 101)
    key_common = jax.random.fold_in(key, 102)
    key_curve = jax.random.fold_in(key, 103)
    key_noise = jax.random.fold_in(key, 104)
    key_align = jax.random.fold_in(key, 105)
    shape = (PAIRS, 3, CELLS_ALL)
    base = jax.random.normal(key_base, shape, jnp.float32)
    common = jax.random.normal(key_common, (3, CELLS_ALL), jnp.float32)
    share = 0.6
    align = jax.random.normal(key_align, (PAIRS, 3), jnp.float32)
    curve = jnp.exp(jax.random.uniform(key_curve, (3, CELLS_ALL), jnp.float32, jnp.log(0.5), jnp.log(5.0)))
    noise = jax.random.normal(key_noise, shape, jnp.float32)
    ramp = 1.0 + 2.0 * jnp.arange(CELLS_ALL, dtype=jnp.float32) / (CELLS_ALL - 1)
    steps = (base + share * common[None] + sizes[None, None, :] * align[:, :, None]) * ramp
    changes = curve[None] * steps + 0.3 * noise * ramp
    return (steps, changes)


def draw_step_pairs(key, part):
    steps, changes = pair_parts(key)
    return steps


def draw_grad_pairs(key, part):
    steps, changes = pair_parts(key)
    return changes


def draw_freq_ids(key, part):
    key = jax.random.fold_in(key, 7)
    key_inner = jax.random.fold_in(key, 1)
    key_place = jax.random.fold_in(key, 2)
    inner = jax.random.permutation(key_inner, NUM_FREQ - 2) + 1
    chosen = jnp.concatenate([jnp.array([0, NUM_FREQ - 1], dtype=jnp.int32), inner[:FREQS - 2].astype(jnp.int32)])
    placed = jax.random.permutation(key_place, chosen)
    return placed.astype(jnp.int32)


def touch_ends(entries, key, smallest, high):
    extent = entries.shape
    spot = [jax.random.randint(jax.random.fold_in(key, axis), (), 0, extent[axis]) for axis in range(len(extent))]
    entries = entries.at[tuple(spot)].set(smallest)
    longest = extent.index(max(extent))
    spot[longest] = (spot[longest] + 1) % extent[longest]
    return entries.at[tuple(spot)].set(high)


def setup_inputs(seed: int = 0) -> dict:
    key_of = jax.random.split(jax.random.key(seed), 10)
    return {
        "forward_field": draw_forward_field(jax.random.fold_in(key_of[9], 71), 0),
        "adjoint_field": draw_adjoint_field(jax.random.fold_in(key_of[9], 71), 0),
        "mass_block": draw_mass_block(jax.random.fold_in(key_of[9], 71), 0),
        "cell_size": draw_cell_size(jax.random.fold_in(key_of[9], 71), 0),
        "freq_weight": jnp.clip(jnp.exp(jax.random.uniform(key_of[4], (NUM_FREQ,), jnp.float32, math.log(0.05), math.log(0.2))), 0.05, 0.2),
        "freq_ids": draw_freq_ids(jax.random.fold_in(key_of[9], 71), 0),
        "receiver_cells": touch_ends(jax.random.randint(key_of[6], (RECEIVERS,), 0, CELLS_ALL), jax.random.fold_in(key_of[6], 1), 0, CELLS_ALL - 1).astype(jnp.int32),
        "step_pairs": draw_step_pairs(jax.random.fold_in(key_of[9], 71), 0),
        "grad_pairs": draw_grad_pairs(jax.random.fold_in(key_of[9], 71), 0),
    }


def contract(forward, adjoint, mass_block):
    fwd = forward.astype(jnp.float32).reshape(2, 3, 4, -1)
    adj = adjoint.astype(jnp.float32).reshape(2, 3, 4, -1)
    coupled = jnp.einsum("kab,pkbc->pkac", mass_block, fwd, precision=lax.Precision.HIGHEST)
    return jnp.sum(adj[0] * coupled[0] - adj[1] * coupled[1], axis=1)


def solve_upper(upper, rhs):
    count = rhs.shape[0]
    places = jnp.arange(count, dtype=jnp.int32)
    result = jnp.zeros_like(rhs)
    for index in range(count - 1, -1, -1):
        value = (rhs[index] - jnp.sum(upper[index] * result)) / upper[index, index]
        result = jnp.where(places == index, value, result)
    return result


def solve_upper_transposed(upper, rhs):
    count = rhs.shape[0]
    places = jnp.arange(count, dtype=jnp.int32)
    result = jnp.zeros_like(rhs)
    for index in range(count):
        value = (rhs[index] - jnp.sum(upper[:, index] * result)) / upper[index, index]
        result = jnp.where(places == index, value, result)
    return result


def quasi_newton(gram, prod, precond, step_pairs, grad_pairs):
    count = step_pairs.shape[0]
    cross = gram[:count, count:]
    grad_gram = gram[count:, count:]
    upper = jnp.triu(cross)
    diagonal = jnp.diagonal(cross)
    gamma = cross[count - 1, count - 1] / grad_gram[count - 1, count - 1]
    first = solve_upper(upper, prod[:count])
    middle = diagonal * first + gamma * jnp.dot(grad_gram, first, precision=lax.Precision.HIGHEST) - gamma * prod[count:]
    second = solve_upper_transposed(upper, middle)
    along_steps = jnp.einsum("m,mkc->kc", second, step_pairs, precision=lax.Precision.HIGHEST)
    along_grads = jnp.einsum("m,mkc->kc", first, grad_pairs, precision=lax.Precision.HIGHEST)
    return -(gamma * precond + along_steps - gamma * along_grads)


def reference(forward_field, adjoint_field, mass_block, cell_size, freq_weight, freq_ids, receiver_cells, step_pairs, grad_pairs):
    slot_weight = freq_weight[freq_ids]

    def one_slot(items):
        forward, adjoint, weight = items
        return (contract(forward, adjoint, mass_block) * weight) * cell_size[None, :]

    sens = lax.map(one_slot, (forward_field, adjoint_field, slot_weight))
    gradient = jnp.sum(sens, axis=0)
    hits = jnp.zeros((CELLS_ALL,), jnp.float32).at[receiver_cells].add(1.0)
    precond = gradient / (1.0 + 4.0 * hits)[None, :]
    stacked = jnp.concatenate([step_pairs, grad_pairs], axis=0).reshape(2 * PAIRS, -1)
    gram = jnp.dot(stacked, stacked.T, precision=lax.Precision.HIGHEST)
    prod = jnp.dot(stacked, precond.reshape(-1), precision=lax.Precision.HIGHEST)
    direction = quasi_newton(gram, prod, precond, step_pairs, grad_pairs)
    predicted = jnp.sum(sens * direction[None], axis=(1, 2)) / PARAMS
    return gradient, direction, predicted
```

```python
import jax
import jax.numpy as jnp
from jax import lax
from jax.experimental import pallas as pl
from jax.experimental.pallas import tpu as pltpu
from jax.sharding import PartitionSpec as P

LANES = 128
PAIRS = 16
SLOTS = 16
EDGES = 12
GROUPS = 16
ROWS = 20
SLAB_ROWS = GROUPS * ROWS
PACK = 64
PER_STEP = 2
FREQ = ("y", "x_lo", "core")
PLANE = ("y", "x_lo", "core", "x_hi")
PARAMS_ALL = 3932160
HIGHEST = lax.Precision.HIGHEST


def sens_kernel(mass, weights, ids, fwd, adj, size, out, mixed):
    rows = PER_STEP * ROWS
    weight = weights[ids[0]]
    scale = size[...]
    for k in range(3):
        for first in range(0, 2 * rows, 16):
            span = slice(first, first + 16)
            e = [fwd[4 * k + b, span, :].astype(jnp.float32) for b in range(4)]
            total = None
            for a in range(4):
                coupled = mass[k * 16 + a * 4] * e[0]
                for b in range(1, 4):
                    coupled = coupled + mass[k * 16 + a * 4 + b] * e[b]
                term = adj[4 * k + a, span, :].astype(jnp.float32) * coupled
                total = term if total is None else total + term
            mixed[k, span, :] = total
        sens = mixed[k, pl.ds(0, rows, stride=2), :] - mixed[k, pl.ds(1, rows, stride=2), :]
        sens = (sens * weight) * scale
        for owner in range(PER_STEP):
            out[owner, k * ROWS : (k + 1) * ROWS, :] = sens[owner * ROWS : (owner + 1) * ROWS, :]


def sens_to_owners(fwd, adj, mass, size, weights, ids):
    smem = pl.BlockSpec(memory_space=pltpu.SMEM)
    rows = PER_STEP * ROWS
    field = pl.BlockSpec((EDGES, 2 * rows, LANES), lambda i: (0, i, 0))
    return pl.pallas_call(
        sens_kernel,
        grid=(GROUPS // PER_STEP,),
        out_shape=jax.ShapeDtypeStruct((GROUPS, PACK, LANES), jnp.float32),
        in_specs=[smem, smem, smem, field, field, pl.BlockSpec((rows, LANES), lambda i: (i, 0))],
        out_specs=pl.BlockSpec((PER_STEP, PACK, LANES), lambda i: (i, 0, 0)),
        scratch_shapes=[pltpu.VMEM((3, 2 * rows, LANES), jnp.float32)],
        compiler_params=pltpu.CompilerParams(vmem_limit_bytes=24 << 20),
        name="sens",
    )(mass, weights, ids, fwd, adj, size)


def products_kernel(cells, sens, steps, grads, gradient, precond, out):
    owner = lax.axis_index(("x_hi", "z")) * GROUPS + lax.axis_index(FREQ)
    offset = cells[...] - owner * (ROWS * LANES)
    inside = (offset >= 0) & (offset < ROWS * LANES)
    row = jnp.where(inside, offset >> 7, -1)
    lane = offset & (LANES - 1)
    row_hot, lane_hot = [], []
    for q in range(8):
        r = jnp.broadcast_to(row[q : q + 1, :], (24, LANES))
        c = jnp.broadcast_to(lane[q : q + 1, :], (LANES, LANES))
        row_hot.append((r == lax.broadcasted_iota(jnp.int32, r.shape, 0)).astype(jnp.float32))
        lane_hot.append((c == lax.broadcasted_iota(jnp.int32, c.shape, 0)).astype(jnp.float32))
    hits = lax.dot_general(
        jnp.concatenate(row_hot, axis=1).astype(jnp.bfloat16),
        jnp.concatenate(lane_hot, axis=1).astype(jnp.bfloat16),
        (((1,), (1,)), ((), ())),
        preferred_element_type=jnp.float32,
    )
    divisor = 1.0 + 4.0 * hits
    products = jnp.zeros((48, 40), jnp.float32)
    for k in range(3):
        slots, damped = [], []
        for r in range(ROWS):
            block = sens[pl.ds(k * ROWS + r, SLOTS, stride=PACK), :]
            span = slice(r * LANES, (r + 1) * LANES)
            total = jnp.sum(block, axis=0, keepdims=True)
            slots.append(block)
            damped.append(total / divisor[r : r + 1, :])
            gradient[k : k + 1, span] = total
            precond[k : k + 1, span] = damped[-1]
        pairs = jnp.concatenate([steps[k], grads[k]], axis=0)
        damped = jnp.broadcast_to(jnp.concatenate(damped, axis=1), (8, ROWS * LANES))
        products = products + lax.dot_general(
            jnp.concatenate([pairs, jnp.concatenate(slots, axis=1)], axis=0),
            jnp.concatenate([pairs, damped], axis=0),
            (((1,), (1,)), ((), ())),
            precision=HIGHEST,
            preferred_element_type=jnp.float32,
        )
    s, y, f = products[:16], products[16:32], products[32:]
    block = jnp.concatenate(
        [s[:, 16:32], y[:, 0:32], f[:, 0:32], s[:, 32:33], y[:, 32:33], f[:, 32:33], jnp.zeros((16, 45), jnp.float32)],
        axis=1,
    )
    for i in range(out.shape[0]):
        out[i] = block


def inner_products(cells, sens, steps, grads, copies):
    vmem = pl.BlockSpec(memory_space=pltpu.VMEM)
    own = jax.ShapeDtypeStruct((3, ROWS * LANES), jnp.float32)
    return pl.pallas_call(
        products_kernel,
        out_shape=(own, own, jax.ShapeDtypeStruct((copies, 16, LANES), jnp.float32)),
        in_specs=[vmem] * 4,
        out_specs=(vmem,) * 3,
        compiler_params=pltpu.CompilerParams(vmem_limit_bytes=24 << 20),
        name="products",
    )(cells, sens, steps, grads)


def resend_kernel(parts, out):
    total = jnp.sum(parts[...], axis=0)
    for i in range(out.shape[0]):
        out[i] = total


def resend(parts, copies):
    vmem = pl.BlockSpec(memory_space=pltpu.VMEM)
    return pl.pallas_call(
        resend_kernel,
        out_shape=jax.ShapeDtypeStruct((copies, 16, LANES), jnp.float32),
        in_specs=[vmem],
        out_specs=vmem,
        name="resend",
    )(parts)


def direction_kernel(parts, steps, grads, precond, direction, predicted):
    block = jnp.sum(parts[...], axis=0)
    row = lax.broadcasted_iota(jnp.int32, (16, LANES), 0)
    lane = lax.broadcasted_iota(jnp.int32, (16, LANES), 1)

    def column(i):
        return jnp.broadcast_to(block[:, i : i + 1], (16, LANES))

    def place(i, value, into):
        return jnp.where(row == i, jnp.broadcast_to(value, (16, LANES)), into)

    diagonal = jnp.sum(jnp.where(row == lane, block, 0.0), axis=1, keepdims=True)
    diagonal = jnp.broadcast_to(diagonal, (16, LANES))
    gamma = jnp.broadcast_to(diagonal[15:16, :] / column(47)[15:16, :], (16, LANES))
    rest = column(80)
    first = jnp.zeros((16, LANES), jnp.float32)
    along = jnp.zeros((16, LANES), jnp.float32)
    slots_first = jnp.zeros((16, LANES), jnp.float32)
    for m in range(15, -1, -1):
        value = rest[m : m + 1, :] / diagonal[m : m + 1, :]
        rest = rest - column(m) * value
        along = along + column(32 + m) * value
        slots_first = slots_first + column(64 + m) * value
        first = place(m, value, first)
    rest = diagonal * first + gamma * along - gamma * column(81)
    second = jnp.zeros((16, LANES), jnp.float32)
    slots_second = jnp.zeros((16, LANES), jnp.float32)
    for m in range(16):
        value = rest[m : m + 1, :] / diagonal[m : m + 1, :]
        rest = rest - column(16 + m) * value
        slots_second = slots_second + column(48 + m) * value
        second = place(m, value, second)
    change = -(gamma * column(82) + slots_second - gamma * slots_first) / PARAMS_ALL
    predicted[...] = jnp.sum(jnp.where(row == lane, change, 0.0), axis=0, keepdims=True)
    scaled = gamma * first
    for k in range(3):
        for r in range(ROWS):
            span = slice(r * LANES, (r + 1) * LANES)
            terms = second * steps[k, :, span] - scaled * grads[k, :, span]
            total = jnp.sum(terms, axis=0, keepdims=True)
            direction[k : k + 1, span] = -(gamma[0:1, :] * precond[k : k + 1, span] + total)


def directions(parts, steps, grads, precond):
    vmem = pl.BlockSpec(memory_space=pltpu.VMEM)
    return pl.pallas_call(
        direction_kernel,
        out_shape=(
            jax.ShapeDtypeStruct((3, ROWS * LANES), jnp.float32),
            jax.ShapeDtypeStruct((1, LANES), jnp.float32),
        ),
        in_specs=[vmem] * 4,
        out_specs=(vmem, vmem),
        name="direction",
    )(parts, steps, grads, precond)


def field_rows(field):
    split = field.reshape(2, EDGES, SLAB_ROWS, LANES)
    return split.transpose(1, 2, 0, 3).reshape(EDGES, 2 * SLAB_ROWS, LANES)


def local(
    forward_field,
    adjoint_field,
    mass_block,
    cell_size,
    freq_weight,
    freq_ids,
    receiver_cells,
    step_pairs,
    grad_pairs,
):
    steps = step_pairs.transpose(1, 0, 2)
    grads = grad_pairs.transpose(1, 0, 2)
    packed = sens_to_owners(
        field_rows(forward_field),
        field_rows(adjoint_field),
        mass_block.reshape(48),
        cell_size.reshape(SLAB_ROWS, LANES),
        freq_weight,
        freq_ids,
    )
    arrived = lax.all_to_all(packed, FREQ, 0, 0, tiled=True)
    gradient, precond, block = inner_products(
        receiver_cells.reshape(8, LANES),
        arrived.reshape(SLOTS * PACK, LANES),
        steps,
        grads,
        lax.axis_size(PLANE),
    )
    parts = lax.all_to_all(block, PLANE, 0, 0, tiled=True)
    parts = lax.all_to_all(resend(parts, lax.axis_size("z")), "z", 0, 0, tiled=True)
    direction, predicted = directions(parts, steps, grads, precond)
    return (gradient, direction, predicted[0, :SLOTS])


def solution(mesh):
    axes = ("y", "x_lo", "core", "x_hi", "z")
    parts = jax.sharding.Mesh(mesh.devices.reshape(4, 2, 2, 2, 16), axes)
    slab = ("x_hi", "z")
    owned = P(None, None, slab + FREQ)
    in_specs = (
        P(FREQ, None, None, slab),
        P(FREQ, None, None, slab),
        P(),
        P(slab),
        P(),
        P(FREQ),
        P(),
        owned,
        owned,
    )
    out_specs = (P(None, slab + FREQ), P(None, slab + FREQ), P())
    return jax.shard_map(local, mesh=parts, in_specs=in_specs, out_specs=out_specs, check_vma=False)
```

```python
import jax
import jax.numpy as jnp
from jax import lax
from jax.experimental import pallas as pl
from jax.experimental.pallas import tpu as pltpu
from jax.sharding import PartitionSpec as P

LANES = 128
PAIRS = 16
SLOTS = 16
EDGES = 12
GROUPS = 16
ROWS = 20
SLAB_ROWS = GROUPS * ROWS
PACK = 64
PER_STEP = 4
FREQ = ("y", "x_lo", "core")
PLANE = ("y", "x_lo", "core", "x_hi")
PARAMS_ALL = 3932160
HIGHEST = lax.Precision.HIGHEST


def sens_kernel(
    ids,
    mass_in,
    weights_in,
    fwd,
    adj,
    size,
    out,
    mass,
    weights,
    e_buf,
    l_buf,
    scale_buf,
    mixed,
    e_sem,
    l_sem,
    small_sem,
):
    rows = PER_STEP * ROWS
    steps = GROUPS // PER_STEP
    small = [
        pltpu.make_async_copy(mass_in, mass, small_sem.at[0]),
        pltpu.make_async_copy(weights_in, weights, small_sem.at[1]),
        pltpu.make_async_copy(size, scale_buf, small_sem.at[2]),
    ]

    def copies(i):
        span = pl.ds(pl.multiple_of(i * 2 * rows, 2 * rows), 2 * rows)
        return (
            pltpu.make_async_copy(fwd.at[:, span, :], e_buf.at[:, span, :], e_sem.at[i]),
            pltpu.make_async_copy(adj.at[:, span, :], l_buf.at[:, span, :], l_sem.at[i]),
        )

    for copy in small:
        copy.start()
    for i in range(steps):
        for copy in copies(i):
            copy.start()
    for copy in small:
        copy.wait()
    weight = weights[ids[0]]

    @pl.loop(0, steps)
    def _(i):
        for copy in copies(i):
            copy.wait()
        scale = scale_buf[pl.ds(pl.multiple_of(i * rows, 8), rows), :]
        for k in range(3):
            for first in range(0, 2 * rows, 16):
                span = pl.ds(pl.multiple_of(i * 2 * rows + first, 16), 16)
                e = [e_buf[4 * k + b, span, :].astype(jnp.float32) for b in range(4)]
                total = None
                for a in range(4):
                    coupled = mass[k, a, 0] * e[0]
                    for b in range(1, 4):
                        coupled = coupled + mass[k, a, b] * e[b]
                    term = l_buf[4 * k + a, span, :].astype(jnp.float32) * coupled
                    total = term if total is None else total + term
                mixed[k, first : first + 16, :] = total
            sens = mixed[k, pl.ds(0, rows, stride=2), :] - mixed[k, pl.ds(1, rows, stride=2), :]
            sens = (sens * weight) * scale
            for owner in range(PER_STEP):
                out[i * PER_STEP + owner, k * ROWS : (k + 1) * ROWS, :] = sens[owner * ROWS : (owner + 1) * ROWS, :]


def sens_to_owners(fwd, adj, mass, size, weights, ids):
    smem = pl.BlockSpec(memory_space=pltpu.SMEM)
    hbm = pl.BlockSpec(memory_space=pltpu.HBM)
    rows = PER_STEP * ROWS
    steps = GROUPS // PER_STEP
    return pl.pallas_call(
        sens_kernel,
        out_shape=jax.ShapeDtypeStruct((GROUPS, PACK, LANES), jnp.float32),
        in_specs=[smem, hbm, hbm, hbm, hbm, hbm],
        out_specs=pl.BlockSpec(memory_space=pltpu.VMEM),
        scratch_shapes=[
            pltpu.SMEM(mass.shape, mass.dtype),
            pltpu.SMEM(weights.shape, weights.dtype),
            pltpu.VMEM(fwd.shape, fwd.dtype),
            pltpu.VMEM(adj.shape, adj.dtype),
            pltpu.VMEM(size.shape, size.dtype),
            pltpu.VMEM((3, 2 * rows, LANES), jnp.float32),
            pltpu.SemaphoreType.DMA((steps,)),
            pltpu.SemaphoreType.DMA((steps,)),
            pltpu.SemaphoreType.DMA((3,)),
        ],
        compiler_params=pltpu.CompilerParams(vmem_limit_bytes=12 << 20),
        name="sens",
    )(ids, *[pltpu.with_memory_space_constraint(each, pltpu.HBM) for each in (mass, weights, fwd, adj, size)])


def products_kernel(cells, sens, steps, grads, gradient_out, precond, out, gradient, gradient_sem):
    owner = lax.axis_index(("x_hi", "z")) * GROUPS + lax.axis_index(FREQ)
    offset = cells[...] - owner * (ROWS * LANES)
    inside = (offset >= 0) & (offset < ROWS * LANES)
    row = jnp.where(inside, offset >> 7, -1)
    lane = offset & (LANES - 1)
    row_hot, lane_hot = [], []
    for q in range(8):
        r = jnp.broadcast_to(row[q : q + 1, :], (24, LANES))
        c = jnp.broadcast_to(lane[q : q + 1, :], (LANES, LANES))
        row_hot.append((r == lax.broadcasted_iota(jnp.int32, r.shape, 0)).astype(jnp.float32))
        lane_hot.append((c == lax.broadcasted_iota(jnp.int32, c.shape, 0)).astype(jnp.float32))
    hits = lax.dot_general(
        jnp.concatenate(row_hot, axis=1).astype(jnp.bfloat16),
        jnp.concatenate(lane_hot, axis=1).astype(jnp.bfloat16),
        (((1,), (1,)), ((), ())),
        preferred_element_type=jnp.float32,
    )
    divisor = 1.0 + 4.0 * hits
    products = jnp.zeros((48, 40), jnp.float32)
    gradient_copy = pltpu.make_async_copy(gradient, gradient_out, gradient_sem)
    for k in range(3):
        slots, damped = [], []
        for r in range(ROWS):
            block = sens[pl.ds(k * ROWS + r, SLOTS, stride=PACK), :]
            span = slice(r * LANES, (r + 1) * LANES)
            total = jnp.sum(block, axis=0, keepdims=True)
            slots.append(block)
            damped.append(total / divisor[r : r + 1, :])
            gradient[k : k + 1, span] = total
            precond[k : k + 1, span] = damped[-1]
        if k == 2:
            gradient_copy.start()
        pairs = jnp.concatenate([steps[k], grads[k]], axis=0)
        damped = jnp.broadcast_to(jnp.concatenate(damped, axis=1), (8, ROWS * LANES))
        products = products + lax.dot_general(
            jnp.concatenate([pairs, jnp.concatenate(slots, axis=1)], axis=0),
            jnp.concatenate([pairs, damped], axis=0),
            (((1,), (1,)), ((), ())),
            precision=HIGHEST,
            preferred_element_type=jnp.float32,
        )
    s, y, f = products[:16], products[16:32], products[32:]
    row = lax.broadcasted_iota(jnp.int32, (16, 16), 0)
    lane = lax.broadcasted_iota(jnp.int32, (16, 16), 1)
    grad_gram = y[:, 16:32]
    block = jnp.concatenate(
        [
            jnp.where(row <= lane, s[:, 16:32], grad_gram),
            jnp.sum(jnp.where(row == lane, grad_gram, 0.0), axis=1, keepdims=True),
            f[:, 0:32],
            s[:, 32:33],
            y[:, 32:33],
            f[:, 32:33],
            jnp.zeros((16, 12), jnp.float32),
        ],
        axis=1,
    )
    block = jnp.concatenate([block[:8], block[8:]], axis=1)
    for i in range(out.shape[0]):
        out[i] = block
    gradient_copy.wait()


def inner_products(cells, sens, steps, grads, copies):
    vmem = pl.BlockSpec(memory_space=pltpu.VMEM)
    own = jax.ShapeDtypeStruct((3, ROWS * LANES), jnp.float32)
    return pl.pallas_call(
        products_kernel,
        out_shape=(own, own, jax.ShapeDtypeStruct((copies, 8, LANES), jnp.float32)),
        in_specs=[vmem] * 4,
        out_specs=(pl.BlockSpec(memory_space=pltpu.HBM), vmem, vmem),
        scratch_shapes=[pltpu.VMEM(own.shape, own.dtype), pltpu.SemaphoreType.DMA(())],
        compiler_params=pltpu.CompilerParams(vmem_limit_bytes=12 << 20),
        name="products",
    )(cells, sens, steps, grads)


def resend_kernel(parts, out):
    total = jnp.sum(parts[...], axis=0)
    for i in range(out.shape[0]):
        out[i] = total


def resend(parts, copies):
    vmem = pl.BlockSpec(memory_space=pltpu.VMEM)
    return pl.pallas_call(
        resend_kernel,
        out_shape=jax.ShapeDtypeStruct((copies, 8, LANES), jnp.float32),
        in_specs=[vmem],
        out_specs=vmem,
        compiler_params=pltpu.CompilerParams(vmem_limit_bytes=4 << 20),
        name="resend",
    )(parts)


def direction_kernel(parts, steps, grads, precond, direction, predicted):
    halves = jnp.sum(parts[...], axis=0)
    block = jnp.concatenate([halves[:, :64], halves[:, 64:]], axis=0)
    turned = jnp.concatenate([block, jnp.zeros((16, 64), jnp.float32)], axis=1)
    turned = jnp.concatenate([turned, jnp.zeros((LANES - 16, LANES), jnp.float32)], axis=0).T[:16]
    row = lax.broadcasted_iota(jnp.int32, (16, LANES), 0)
    lane = lax.broadcasted_iota(jnp.int32, (16, LANES), 1)

    def column(i, of=block):
        return jnp.broadcast_to(of[:, i : i + 1], (16, LANES))

    def place(i, value, into):
        return jnp.where(row == i, jnp.broadcast_to(value, (16, LANES)), into)

    diagonal = jnp.where(row[:, :64] == lane[:, :64], block, 0.0)
    diagonal = jnp.broadcast_to(jnp.sum(diagonal, axis=1, keepdims=True), (16, LANES))
    grad_diagonal = column(16)
    gamma = jnp.broadcast_to(diagonal[15:16, :] / grad_diagonal[15:16, :], (16, LANES))
    rest = column(49)
    first = jnp.zeros((16, LANES), jnp.float32)
    along = jnp.zeros((16, LANES), jnp.float32)
    slots_first = jnp.zeros((16, LANES), jnp.float32)
    for m in range(15, -1, -1):
        value = rest[m : m + 1, :] / diagonal[m : m + 1, :]
        upper = column(m)
        rest = rest - upper * value
        grad_column = jnp.where(row > m, upper, jnp.where(row < m, column(m, turned), grad_diagonal))
        along = along + grad_column * value
        slots_first = slots_first + column(33 + m) * value
        first = place(m, value, first)
    rest = diagonal * first + gamma * along - gamma * column(50)
    second = jnp.zeros((16, LANES), jnp.float32)
    slots_second = jnp.zeros((16, LANES), jnp.float32)
    for m in range(16):
        value = rest[m : m + 1, :] / diagonal[m : m + 1, :]
        rest = rest - column(m, turned) * value
        slots_second = slots_second + column(17 + m) * value
        second = place(m, value, second)
    change = -(gamma * column(51) + slots_second - gamma * slots_first) / PARAMS_ALL
    predicted[...] = jnp.sum(jnp.where(row == lane, change, 0.0), axis=0)[:SLOTS]
    scaled = gamma * first
    for k in range(3):
        for r in range(ROWS):
            span = slice(r * LANES, (r + 1) * LANES)
            terms = second * steps[k, :, span] - scaled * grads[k, :, span]
            total = jnp.sum(terms, axis=0, keepdims=True)
            direction[k : k + 1, span] = -(gamma[0:1, :] * precond[k : k + 1, span] + total)


def directions(parts, steps, grads, precond):
    vmem = pl.BlockSpec(memory_space=pltpu.VMEM)
    return pl.pallas_call(
        direction_kernel,
        out_shape=(
            jax.ShapeDtypeStruct((3, ROWS * LANES), jnp.float32),
            jax.ShapeDtypeStruct((SLOTS,), jnp.float32),
        ),
        in_specs=[vmem] * 4,
        out_specs=(vmem, vmem),
        compiler_params=pltpu.CompilerParams(vmem_limit_bytes=8 << 20),
        name="direction",
    )(parts, steps, grads, precond)


def field_rows(field):
    split = field.reshape(2, EDGES, SLAB_ROWS, LANES)
    return split.transpose(1, 2, 0, 3).reshape(EDGES, 2 * SLAB_ROWS, LANES)


def local(
    forward_field,
    adjoint_field,
    mass_block,
    cell_size,
    freq_weight,
    freq_ids,
    receiver_cells,
    step_pairs,
    grad_pairs,
):
    steps = step_pairs.transpose(1, 0, 2)
    grads = grad_pairs.transpose(1, 0, 2)
    packed = sens_to_owners(
        field_rows(forward_field),
        field_rows(adjoint_field),
        mass_block,
        cell_size.reshape(SLAB_ROWS, LANES),
        freq_weight,
        freq_ids,
    )
    arrived = lax.all_to_all(packed, FREQ, 0, 0, tiled=True)
    gradient, precond, block = inner_products(
        receiver_cells.reshape(8, LANES),
        arrived.reshape(SLOTS * PACK, LANES),
        steps,
        grads,
        lax.axis_size(PLANE),
    )
    parts = lax.all_to_all(block, PLANE, 0, 0, tiled=True)
    parts = lax.all_to_all(resend(parts, lax.axis_size("z")), "z", 0, 0, tiled=True)
    direction, predicted = directions(parts, steps, grads, precond)
    return (gradient, direction, predicted)


def solution(mesh):
    axes = ("y", "x_lo", "core", "x_hi", "z")
    parts = jax.sharding.Mesh(mesh.devices.reshape(4, 2, 2, 2, 16), axes)
    slab = ("x_hi", "z")
    owned = P(None, None, slab + FREQ)
    in_specs = (
        P(FREQ, None, None, slab),
        P(FREQ, None, None, slab),
        P(),
        P(slab),
        P(),
        P(FREQ),
        P(),
        owned,
        owned,
    )
    out_specs = (P(None, slab + FREQ), P(None, slab + FREQ), P())
    return jax.shard_map(local, mesh=parts, in_specs=in_specs, out_specs=out_specs, check_vma=False)
```

```python
import jax
import jax.numpy as jnp
from jax import lax
from jax.experimental import pallas as pl
from jax.experimental.pallas import tpu as pltpu
from jax.sharding import PartitionSpec as P

LANES = 128
PAIRS = 16
SLOTS = 16
EDGES = 12
GROUPS = 16
ROWS = 20
SLAB_ROWS = GROUPS * ROWS
PACK = 64
PER_STEP = 4
FREQ = ("y", "x_lo", "core")
PLANE = ("y", "x_lo", "core", "x_hi")
PARAMS_ALL = 3932160
HIGHEST = lax.Precision.HIGHEST


def sens_kernel(
    ids,
    mass_in,
    weights_in,
    fwd,
    adj,
    size,
    out,
    mass,
    weights,
    e_buf,
    l_buf,
    scale_buf,
    mixed,
    e_sem,
    l_sem,
    small_sem,
):
    rows = PER_STEP * ROWS
    steps = GROUPS // PER_STEP
    small = [
        pltpu.make_async_copy(mass_in, mass, small_sem.at[0]),
        pltpu.make_async_copy(weights_in, weights, small_sem.at[1]),
        pltpu.make_async_copy(size, scale_buf, small_sem.at[2]),
    ]

    def copies(i):
        span = pl.ds(pl.multiple_of(i * 2 * rows, 2 * rows), 2 * rows)
        return (
            pltpu.make_async_copy(fwd.at[:, span, :], e_buf.at[:, span, :], e_sem.at[i]),
            pltpu.make_async_copy(adj.at[:, span, :], l_buf.at[:, span, :], l_sem.at[i]),
        )

    for copy in small:
        copy.start()
    for i in range(steps):
        for copy in copies(i):
            copy.start()
    for copy in small:
        copy.wait()
    weight = weights[ids[0]]

    @pl.loop(0, steps)
    def _(i):
        for copy in copies(i):
            copy.wait()
        scale = scale_buf[pl.ds(pl.multiple_of(i * rows, 8), rows), :]
        for k in range(3):
            for first in range(0, 2 * rows, 16):
                span = pl.ds(pl.multiple_of(i * 2 * rows + first, 16), 16)
                e = [e_buf[4 * k + b, span, :].astype(jnp.float32) for b in range(4)]
                total = None
                for a in range(4):
                    coupled = mass[k, a, 0] * e[0]
                    for b in range(1, 4):
                        coupled = coupled + mass[k, a, b] * e[b]
                    term = l_buf[4 * k + a, span, :].astype(jnp.float32) * coupled
                    total = term if total is None else total + term
                mixed[k, first : first + 16, :] = total
            sens = mixed[k, pl.ds(0, rows, stride=2), :] - mixed[k, pl.ds(1, rows, stride=2), :]
            sens = (sens * weight) * scale
            for owner in range(PER_STEP):
                out[i * PER_STEP + owner, k * ROWS : (k + 1) * ROWS, :] = sens[owner * ROWS : (owner + 1) * ROWS, :]


def sens_to_owners(fwd, adj, mass, size, weights, ids):
    smem = pl.BlockSpec(memory_space=pltpu.SMEM)
    hbm = pl.BlockSpec(memory_space=pltpu.HBM)
    rows = PER_STEP * ROWS
    steps = GROUPS // PER_STEP
    return pl.pallas_call(
        sens_kernel,
        out_shape=jax.ShapeDtypeStruct((GROUPS, PACK, LANES), jnp.float32),
        in_specs=[smem, hbm, hbm, hbm, hbm, hbm],
        out_specs=pl.BlockSpec(memory_space=pltpu.VMEM),
        scratch_shapes=[
            pltpu.SMEM(mass.shape, mass.dtype),
            pltpu.SMEM(weights.shape, weights.dtype),
            pltpu.VMEM(fwd.shape, fwd.dtype),
            pltpu.VMEM(adj.shape, adj.dtype),
            pltpu.VMEM(size.shape, size.dtype),
            pltpu.VMEM((3, 2 * rows, LANES), jnp.float32),
            pltpu.SemaphoreType.DMA((steps,)),
            pltpu.SemaphoreType.DMA((steps,)),
            pltpu.SemaphoreType.DMA((3,)),
        ],
        compiler_params=pltpu.CompilerParams(vmem_limit_bytes=12 << 20),
        name="sens",
    )(ids, *[pltpu.with_memory_space_constraint(each, pltpu.HBM) for each in (mass, weights, fwd, adj, size)])


def products_kernel(cells, sens, steps, grads, gradient_out, precond, out, gradient, gradient_sem):
    owner = lax.axis_index(("x_hi", "z")) * GROUPS + lax.axis_index(FREQ)
    offset = cells[...] - owner * (ROWS * LANES)
    inside = (offset >= 0) & (offset < ROWS * LANES)
    row = jnp.where(inside, offset >> 7, -1)
    lane = offset & (LANES - 1)
    row_hot, lane_hot = [], []
    for q in range(8):
        r = jnp.broadcast_to(row[q : q + 1, :], (24, LANES))
        c = jnp.broadcast_to(lane[q : q + 1, :], (LANES, LANES))
        row_hot.append((r == lax.broadcasted_iota(jnp.int32, r.shape, 0)).astype(jnp.float32))
        lane_hot.append((c == lax.broadcasted_iota(jnp.int32, c.shape, 0)).astype(jnp.float32))
    hits = lax.dot_general(
        jnp.concatenate(row_hot, axis=1).astype(jnp.bfloat16),
        jnp.concatenate(lane_hot, axis=1).astype(jnp.bfloat16),
        (((1,), (1,)), ((), ())),
        preferred_element_type=jnp.float32,
    )
    divisor = 1.0 + 4.0 * hits
    products = jnp.zeros((48, 40), jnp.float32)
    gradient_copy = pltpu.make_async_copy(gradient, gradient_out, gradient_sem)
    for k in range(3):
        slots, damped = [], []
        for r in range(ROWS):
            block = sens[pl.ds(k * ROWS + r, SLOTS, stride=PACK), :]
            span = slice(r * LANES, (r + 1) * LANES)
            total = jnp.sum(block, axis=0, keepdims=True)
            slots.append(block)
            damped.append(total / divisor[r : r + 1, :])
            gradient[k : k + 1, span] = total
            precond[k : k + 1, span] = damped[-1]
        if k == 2:
            gradient_copy.start()
        pairs = jnp.concatenate([steps[k], grads[k]], axis=0)
        damped = jnp.broadcast_to(jnp.concatenate(damped, axis=1), (8, ROWS * LANES))
        products = products + lax.dot_general(
            jnp.concatenate([pairs, jnp.concatenate(slots, axis=1)], axis=0),
            jnp.concatenate([pairs, damped], axis=0),
            (((1,), (1,)), ((), ())),
            precision=HIGHEST,
            preferred_element_type=jnp.float32,
        )
    s, y, f = products[:16], products[16:32], products[32:]
    row = lax.broadcasted_iota(jnp.int32, (16, 16), 0)
    lane = lax.broadcasted_iota(jnp.int32, (16, 16), 1)
    grad_gram = y[:, 16:32]
    block = jnp.concatenate(
        [
            jnp.where(row <= lane, s[:, 16:32], grad_gram),
            jnp.sum(jnp.where(row == lane, grad_gram, 0.0), axis=1, keepdims=True),
            f[:, 0:32],
            s[:, 32:33],
            y[:, 32:33],
            f[:, 32:33],
            jnp.zeros((16, 12), jnp.float32),
        ],
        axis=1,
    )
    block = jnp.concatenate([block[:8], block[8:]], axis=1)
    for i in range(out.shape[0]):
        out[i] = block
    gradient_copy.wait()


def inner_products(cells, sens, steps, grads, copies):
    vmem = pl.BlockSpec(memory_space=pltpu.VMEM)
    own = jax.ShapeDtypeStruct((3, ROWS * LANES), jnp.float32)
    return pl.pallas_call(
        products_kernel,
        out_shape=(own, own, jax.ShapeDtypeStruct((copies, 8, LANES), jnp.float32)),
        in_specs=[vmem] * 4,
        out_specs=(pl.BlockSpec(memory_space=pltpu.HBM), vmem, vmem),
        scratch_shapes=[pltpu.VMEM(own.shape, own.dtype), pltpu.SemaphoreType.DMA(())],
        compiler_params=pltpu.CompilerParams(vmem_limit_bytes=12 << 20),
        name="products",
    )(cells, sens, steps, grads)


def resend_kernel(parts, out):
    total = jnp.sum(parts[...], axis=0)
    for i in range(out.shape[0]):
        out[i] = total


def resend(parts, copies):
    vmem = pl.BlockSpec(memory_space=pltpu.VMEM)
    return pl.pallas_call(
        resend_kernel,
        out_shape=jax.ShapeDtypeStruct((copies, 8, LANES), jnp.float32),
        in_specs=[vmem],
        out_specs=vmem,
        compiler_params=pltpu.CompilerParams(vmem_limit_bytes=4 << 20),
        name="resend",
    )(parts)


def direction_kernel(parts, steps, grads, precond, direction, predicted):
    halves = jnp.sum(parts[...], axis=0)
    block = jnp.concatenate([halves[:, :64], halves[:, 64:]], axis=0)
    turned = jnp.concatenate([block, jnp.zeros((16, 64), jnp.float32)], axis=1)
    turned = jnp.concatenate([turned, jnp.zeros((LANES - 16, LANES), jnp.float32)], axis=0).T[:16]
    row = lax.broadcasted_iota(jnp.int32, (16, LANES), 0)
    lane = lax.broadcasted_iota(jnp.int32, (16, LANES), 1)

    def column(i, of=block):
        return jnp.broadcast_to(of[:, i : i + 1], (16, LANES))

    def place(i, value, into):
        return jnp.where(row == i, jnp.broadcast_to(value, (16, LANES)), into)

    diagonal = jnp.where(row[:, :64] == lane[:, :64], block, 0.0)
    diagonal = jnp.broadcast_to(jnp.sum(diagonal, axis=1, keepdims=True), (16, LANES))
    grad_diagonal = column(16)
    gamma = jnp.broadcast_to(diagonal[15:16, :] / grad_diagonal[15:16, :], (16, LANES))
    rest = column(49)
    first = jnp.zeros((16, LANES), jnp.float32)
    along = jnp.zeros((16, LANES), jnp.float32)
    slots_first = jnp.zeros((16, LANES), jnp.float32)
    for m in range(15, -1, -1):
        value = rest[m : m + 1, :] / diagonal[m : m + 1, :]
        upper = column(m)
        rest = rest - upper * value
        grad_column = jnp.where(row > m, upper, jnp.where(row < m, column(m, turned), grad_diagonal))
        along = along + grad_column * value
        slots_first = slots_first + column(33 + m) * value
        first = place(m, value, first)
    rest = diagonal * first + gamma * along - gamma * column(50)
    second = jnp.zeros((16, LANES), jnp.float32)
    slots_second = jnp.zeros((16, LANES), jnp.float32)
    for m in range(16):
        value = rest[m : m + 1, :] / diagonal[m : m + 1, :]
        rest = rest - column(m, turned) * value
        slots_second = slots_second + column(17 + m) * value
        second = place(m, value, second)
    change = -(gamma * column(51) + slots_second - gamma * slots_first) / PARAMS_ALL
    predicted[...] = jnp.sum(jnp.where(row == lane, change, 0.0), axis=0)[:SLOTS]
    scaled = gamma * first
    for k in range(3):
        for r in range(ROWS):
            span = slice(r * LANES, (r + 1) * LANES)
            terms = second * steps[k, :, span] - scaled * grads[k, :, span]
            total = jnp.sum(terms, axis=0, keepdims=True)
            direction[k : k + 1, span] = -(gamma[0:1, :] * precond[k : k + 1, span] + total)


def directions(parts, steps, grads, precond):
    vmem = pl.BlockSpec(memory_space=pltpu.VMEM)
    return pl.pallas_call(
        direction_kernel,
        out_shape=(
            jax.ShapeDtypeStruct((3, ROWS * LANES), jnp.float32),
            jax.ShapeDtypeStruct((SLOTS,), jnp.float32),
        ),
        in_specs=[vmem] * 4,
        out_specs=(vmem, vmem),
        compiler_params=pltpu.CompilerParams(vmem_limit_bytes=8 << 20),
        name="direction",
    )(parts, steps, grads, precond)


def field_rows(field):
    split = field.reshape(2, EDGES, SLAB_ROWS, LANES)
    return split.transpose(1, 2, 0, 3).reshape(EDGES, 2 * SLAB_ROWS, LANES)


def local(
    forward_field,
    adjoint_field,
    mass_block,
    cell_size,
    freq_weight,
    freq_ids,
    receiver_cells,
    step_pairs,
    grad_pairs,
):
    steps = step_pairs.transpose(1, 0, 2)
    grads = grad_pairs.transpose(1, 0, 2)
    packed = sens_to_owners(
        field_rows(forward_field),
        field_rows(adjoint_field),
        mass_block,
        cell_size.reshape(SLAB_ROWS, LANES),
        freq_weight,
        freq_ids,
    )
    arrived = lax.all_to_all(packed, FREQ, 0, 0, tiled=True)
    gradient, precond, block = inner_products(
        receiver_cells.reshape(8, LANES),
        arrived.reshape(SLOTS * PACK, LANES),
        steps,
        grads,
        lax.axis_size(PLANE),
    )
    parts = lax.all_to_all(block, PLANE, 0, 0, tiled=True)
    parts = lax.all_to_all(resend(parts, lax.axis_size("z")), "z", 0, 0, tiled=True, axis_index_groups=[[(i+8)%16 for i in range(16)]])
    direction, predicted = directions(parts, steps, grads, precond)
    return (gradient, direction, predicted)


def solution(mesh):
    axes = ("y", "x_lo", "core", "x_hi", "z")
    parts = jax.sharding.Mesh(mesh.devices.reshape(4, 2, 2, 2, 16), axes)
    slab = ("x_hi", "z")
    owned = P(None, None, slab + FREQ)
    in_specs = (
        P(FREQ, None, None, slab),
        P(FREQ, None, None, slab),
        P(),
        P(slab),
        P(),
        P(FREQ),
        P(),
        owned,
        owned,
    )
    out_specs = (P(None, slab + FREQ), P(None, slab + FREQ), P())
    return jax.shard_map(local, mesh=parts, in_specs=in_specs, out_specs=out_specs, check_vma=False)
```

```python
import jax
import jax.numpy as jnp
from jax import lax
from jax.experimental import pallas as pl
from jax.experimental.pallas import tpu as pltpu
from jax.sharding import PartitionSpec as P

LANES = 128
PAIRS = 16
SLOTS = 16
EDGES = 12
GROUPS = 16
ROWS = 20
SLAB_ROWS = GROUPS * ROWS
PACK = 64
PER_STEP = 4
FREQ = ("y", "x_lo", "core")
PLANE = ("y", "x_lo", "core", "x_hi")
PARAMS_ALL = 3932160
SPLITS = 3


def sens_kernel(
    ids,
    mass_in,
    weights_in,
    fwd,
    adj,
    size,
    out,
    mass,
    weights,
    e_buf,
    l_buf,
    scale_buf,
    mixed,
    e_sem,
    l_sem,
    small_sem,
):
    rows = PER_STEP * ROWS
    steps = GROUPS // PER_STEP
    small = [
        pltpu.make_async_copy(mass_in, mass, small_sem.at[0]),
        pltpu.make_async_copy(weights_in, weights, small_sem.at[1]),
        pltpu.make_async_copy(size, scale_buf, small_sem.at[2]),
    ]

    def copies(i):
        span = pl.ds(pl.multiple_of(i * 2 * rows, 2 * rows), 2 * rows)
        return (
            pltpu.make_async_copy(fwd.at[:, span, :], e_buf.at[:, span, :], e_sem.at[i]),
            pltpu.make_async_copy(adj.at[:, span, :], l_buf.at[:, span, :], l_sem.at[i]),
        )

    for copy in small:
        copy.start()
    for i in range(steps):
        for copy in copies(i):
            copy.start()
    for copy in small:
        copy.wait()
    weight = weights[ids[0]]

    @pl.loop(0, steps)
    def _(i):
        for copy in copies(i):
            copy.wait()
        scale = scale_buf[pl.ds(pl.multiple_of(i * rows, 8), rows), :] * weight
        for k in range(3):
            for first in range(0, 2 * rows, 16):
                span = pl.ds(pl.multiple_of(i * 2 * rows + first, 16), 16)
                e = [e_buf[4 * k + b, span, :].astype(jnp.float32) for b in range(4)]
                total = None
                for a in range(4):
                    coupled = mass[k, a, 0] * e[0]
                    for b in range(1, 4):
                        coupled = coupled + mass[k, a, b] * e[b]
                    term = l_buf[4 * k + a, span, :].astype(jnp.float32) * coupled
                    total = term if total is None else total + term
                mixed[k, first : first + 16, :] = total
        for k in range(3):
            sens = mixed[k, pl.ds(0, rows, stride=2), :] - mixed[k, pl.ds(1, rows, stride=2), :]
            sens = sens * scale
            for owner in range(PER_STEP):
                out[i * PER_STEP + owner, k * ROWS : (k + 1) * ROWS, :] = sens[owner * ROWS : (owner + 1) * ROWS, :]


def sens_to_owners(fwd, adj, mass, size, weights, ids):
    smem = pl.BlockSpec(memory_space=pltpu.SMEM)
    hbm = pl.BlockSpec(memory_space=pltpu.HBM)
    rows = PER_STEP * ROWS
    steps = GROUPS // PER_STEP
    return pl.pallas_call(
        sens_kernel,
        out_shape=jax.ShapeDtypeStruct((GROUPS, PACK, LANES), jnp.float32),
        in_specs=[smem, hbm, hbm, hbm, hbm, hbm],
        out_specs=pl.BlockSpec(memory_space=pltpu.VMEM),
        scratch_shapes=[
            pltpu.SMEM(mass.shape, mass.dtype),
            pltpu.SMEM(weights.shape, weights.dtype),
            pltpu.VMEM(fwd.shape, fwd.dtype),
            pltpu.VMEM(adj.shape, adj.dtype),
            pltpu.VMEM(size.shape, size.dtype),
            pltpu.VMEM((3, 2 * rows, LANES), jnp.float32),
            pltpu.SemaphoreType.DMA((steps,)),
            pltpu.SemaphoreType.DMA((steps,)),
            pltpu.SemaphoreType.DMA((3,)),
        ],
        compiler_params=pltpu.CompilerParams(vmem_limit_bytes=12 << 20),
        name="sens",
    )(ids, *[pltpu.with_memory_space_constraint(each, pltpu.HBM) for each in (mass, weights, fwd, adj, size)])


def split(values):
    parts = []
    for _ in range(SPLITS):
        parts.append(values.astype(jnp.bfloat16))
        values = values - parts[-1].astype(jnp.float32)
    return parts


def products_kernel(
    cells, sens, steps, grads, gradient_out, precond, out, gradient, total_rows, damped_rows, gradient_sem
):
    owner = lax.axis_index(("x_hi", "z")) * GROUPS + lax.axis_index(FREQ)
    offset = cells[...] - owner * (ROWS * LANES)
    inside = (offset >= 0) & (offset < ROWS * LANES)
    row = jnp.where(inside, offset >> 7, -1)
    lane = offset & (LANES - 1)
    place = lax.broadcasted_iota(jnp.int32, (PACK, LANES), 0)
    place = jnp.where(place < 2 * ROWS, jnp.where(place < ROWS, place, place - ROWS), place - 2 * ROWS)
    column = lax.broadcasted_iota(jnp.int32, (LANES, LANES), 0)
    row_hot, lane_hot = [], []
    for q in range(8):
        row_hot.append((row[q : q + 1, :] == place).astype(jnp.float32).astype(jnp.bfloat16))
        lane_hot.append((lane[q : q + 1, :] == column).astype(jnp.float32).astype(jnp.bfloat16))
    hits = lax.dot_general(
        jnp.concatenate(row_hot, axis=1),
        jnp.concatenate(lane_hot, axis=1),
        (((1,), (1,)), ((), ())),
        preferred_element_type=jnp.float32,
    )
    total = sens[0:PACK, :]
    for f in range(1, SLOTS):
        total = total + sens[f * PACK : (f + 1) * PACK, :]
    total_rows[...] = total
    for r in range(ROWS):
        gradient[:, r * LANES : (r + 1) * LANES] = total_rows[pl.ds(r, 3, stride=ROWS), :]
    gradient_copy = pltpu.make_async_copy(gradient, gradient_out, gradient_sem)
    gradient_copy.start()
    damped_rows[...] = total / (1.0 + 4.0 * hits)
    for r in range(ROWS):
        precond[:, r * LANES : (r + 1) * LANES] = damped_rows[pl.ds(r, 3, stride=ROWS), :]
    products = jnp.zeros((144, 144), jnp.float32)
    for k in range(3):
        slots, damped = [], []
        for r in range(ROWS):
            slots.append(sens[pl.ds(k * ROWS + r, SLOTS, stride=PACK), :])
            damped.append(jnp.broadcast_to(damped_rows[k * ROWS + r : k * ROWS + r + 1, :], (16, LANES)))
        pairs = split(jnp.concatenate([steps[k], grads[k]], axis=0))
        slots = split(jnp.concatenate(slots, axis=1))
        damped = split(jnp.concatenate(damped, axis=1))
        products = products + lax.dot_general(
            jnp.concatenate([*pairs, *slots], axis=0),
            jnp.concatenate([*pairs, *damped], axis=0),
            (((1,), (1,)), ((), ())),
            preferred_element_type=jnp.float32,
        )
    products = sum(
        products[:, 32 * b : 32 * b + 32] for b in reversed(range(SPLITS))
    ), sum(products[:, 32 * SPLITS + 16 * b : 32 * SPLITS + 16 * b + 16] for b in reversed(range(SPLITS)))
    products = jnp.concatenate(products, axis=1)
    products = jnp.concatenate(
        [
            sum(products[32 * a : 32 * a + 32] for a in reversed(range(SPLITS))),
            sum(products[32 * SPLITS + 16 * a : 32 * SPLITS + 16 * a + 16] for a in reversed(range(SPLITS))),
        ],
        axis=0,
    )
    s, y, f = products[:16], products[16:32], products[32:]
    row = lax.broadcasted_iota(jnp.int32, (16, 16), 0)
    lane = lax.broadcasted_iota(jnp.int32, (16, 16), 1)
    grad_gram = y[:, 16:32]
    block = jnp.concatenate(
        [
            jnp.where(row <= lane, s[:, 16:32], grad_gram),
            jnp.sum(jnp.where(row == lane, grad_gram, 0.0), axis=1, keepdims=True),
            f[:, 0:32],
            s[:, 32:33],
            y[:, 32:33],
            f[:, 32:33],
            jnp.zeros((16, 12), jnp.float32),
        ],
        axis=1,
    )
    block = jnp.concatenate([block[:8], block[8:]], axis=1)
    for i in range(out.shape[0]):
        out[i] = block
    gradient_copy.wait()


def inner_products(cells, sens, steps, grads, copies):
    vmem = pl.BlockSpec(memory_space=pltpu.VMEM)
    own = jax.ShapeDtypeStruct((3, ROWS * LANES), jnp.float32)
    return pl.pallas_call(
        products_kernel,
        out_shape=(own, own, jax.ShapeDtypeStruct((copies, 8, LANES), jnp.float32)),
        in_specs=[vmem] * 4,
        out_specs=(pl.BlockSpec(memory_space=pltpu.HBM), vmem, vmem),
        scratch_shapes=[
            pltpu.VMEM(own.shape, own.dtype),
            pltpu.VMEM((PACK, LANES), jnp.float32),
            pltpu.VMEM((PACK, LANES), jnp.float32),
            pltpu.SemaphoreType.DMA(()),
        ],
        compiler_params=pltpu.CompilerParams(vmem_limit_bytes=12 << 20),
        name="products",
    )(cells, sens, steps, grads)


def resend_kernel(parts, out):
    total = jnp.sum(parts[...], axis=0)
    for i in range(out.shape[0]):
        out[i] = total


def resend(parts, copies):
    vmem = pl.BlockSpec(memory_space=pltpu.VMEM)
    return pl.pallas_call(
        resend_kernel,
        out_shape=jax.ShapeDtypeStruct((copies, 8, LANES), jnp.float32),
        in_specs=[vmem],
        out_specs=vmem,
        compiler_params=pltpu.CompilerParams(vmem_limit_bytes=4 << 20),
        name="resend",
    )(parts)


def direction_kernel(parts, steps, grads, precond, direction, predicted):
    halves = jnp.sum(parts[...], axis=0)
    block = jnp.concatenate([halves[:, :64], halves[:, 64:]], axis=0)
    turned = jnp.concatenate([block, jnp.zeros((16, 64), jnp.float32)], axis=1)
    turned = jnp.concatenate([turned, jnp.zeros((LANES - 16, LANES), jnp.float32)], axis=0).T[:16]
    row = lax.broadcasted_iota(jnp.int32, (16, LANES), 0)
    lane = lax.broadcasted_iota(jnp.int32, (16, LANES), 1)

    def column(i, of=block):
        return jnp.broadcast_to(of[:, i : i + 1], (16, LANES))

    def place(i, value, into):
        return jnp.where(row == i, jnp.broadcast_to(value, (16, LANES)), into)

    diagonal = jnp.where(row[:, :64] == lane[:, :64], block, 0.0)
    diagonal = jnp.broadcast_to(jnp.sum(diagonal, axis=1, keepdims=True), (16, LANES))
    grad_diagonal = column(16)
    gamma = jnp.broadcast_to(diagonal[15:16, :] / grad_diagonal[15:16, :], (16, LANES))
    rest = column(49)
    first = jnp.zeros((16, LANES), jnp.float32)
    along = jnp.zeros((16, LANES), jnp.float32)
    slots_first = jnp.zeros((16, LANES), jnp.float32)
    for m in range(15, -1, -1):
        value = rest[m : m + 1, :] / diagonal[m : m + 1, :]
        upper = column(m)
        rest = rest - upper * value
        grad_column = jnp.where(row > m, upper, jnp.where(row < m, column(m, turned), grad_diagonal))
        along = along + grad_column * value
        slots_first = slots_first + column(33 + m) * value
        first = place(m, value, first)
    rest = diagonal * first + gamma * along - gamma * column(50)
    second = jnp.zeros((16, LANES), jnp.float32)
    slots_second = jnp.zeros((16, LANES), jnp.float32)
    for m in range(16):
        value = rest[m : m + 1, :] / diagonal[m : m + 1, :]
        rest = rest - column(m, turned) * value
        slots_second = slots_second + column(17 + m) * value
        second = place(m, value, second)
    change = -(gamma * column(51) + slots_second - gamma * slots_first) / PARAMS_ALL
    predicted[...] = jnp.sum(jnp.where(row == lane, change, 0.0), axis=0)[:SLOTS]
    scaled = gamma * first
    for k in range(3):
        for r in range(ROWS):
            span = slice(r * LANES, (r + 1) * LANES)
            terms = second * steps[k, :, span] - scaled * grads[k, :, span]
            total = jnp.sum(terms, axis=0, keepdims=True)
            direction[k : k + 1, span] = -(gamma[0:1, :] * precond[k : k + 1, span] + total)


def directions(parts, steps, grads, precond):
    vmem = pl.BlockSpec(memory_space=pltpu.VMEM)
    own = jax.ShapeDtypeStruct((3, ROWS * LANES), jnp.float32)
    return pl.pallas_call(
        direction_kernel,
        out_shape=(own, jax.ShapeDtypeStruct((SLOTS,), jnp.float32)),
        in_specs=[vmem] * 4,
        out_specs=(vmem, vmem),
        compiler_params=pltpu.CompilerParams(vmem_limit_bytes=8 << 20),
        name="direction",
    )(parts, steps, grads, precond)


def field_rows(field):
    split = field.reshape(2, EDGES, SLAB_ROWS, LANES)
    return split.transpose(1, 2, 0, 3).reshape(EDGES, 2 * SLAB_ROWS, LANES)


def local(
    forward_field,
    adjoint_field,
    mass_block,
    cell_size,
    freq_weight,
    freq_ids,
    receiver_cells,
    step_pairs,
    grad_pairs,
):
    steps = step_pairs.transpose(1, 0, 2)
    grads = grad_pairs.transpose(1, 0, 2)
    packed = sens_to_owners(
        field_rows(forward_field),
        field_rows(adjoint_field),
        mass_block,
        cell_size.reshape(SLAB_ROWS, LANES),
        freq_weight,
        freq_ids,
    )
    arrived = lax.all_to_all(packed, FREQ, 0, 0, tiled=True)
    gradient, precond, block = inner_products(
        receiver_cells.reshape(8, LANES),
        arrived.reshape(SLOTS * PACK, LANES),
        steps,
        grads,
        lax.axis_size(PLANE),
    )
    parts = lax.all_to_all(block, PLANE, 0, 0, tiled=True, axis_index_groups=[[(i + 14) % 32 for i in range(32)]])
    parts = lax.all_to_all(resend(parts, lax.axis_size("z")), "z", 0, 0, tiled=True, axis_index_groups=[[(i+8)%16 for i in range(16)]])
    direction, predicted = directions(parts, steps, grads, precond)
    return (gradient, direction, predicted)


def solution(mesh):
    axes = ("y", "x_lo", "core", "x_hi", "z")
    parts = jax.sharding.Mesh(mesh.devices.reshape(4, 2, 2, 2, 16), axes)
    slab = ("x_hi", "z")
    owned = P(None, None, slab + FREQ)
    in_specs = (
        P(FREQ, None, None, slab),
        P(FREQ, None, None, slab),
        P(),
        P(slab),
        P(),
        P(FREQ),
        P(),
        owned,
        owned,
    )
    out_specs = (P(None, slab + FREQ), P(None, slab + FREQ), P())
    return jax.shard_map(local, mesh=parts, in_specs=in_specs, out_specs=out_specs, check_vma=False)
```

```python
import jax
import jax.numpy as jnp
from jax import lax
from jax.experimental import pallas as pl
from jax.experimental.pallas import tpu as pltpu
from jax.sharding import PartitionSpec as P

LANES = 128
PAIRS = 16
SLOTS = 16
EDGES = 12
GROUPS = 16
ROWS = 20
SLAB_ROWS = GROUPS * ROWS
PACK = 64
PER_STEP = 4
FREQ = ("y", "x_lo", "core")
PLANE = ("y", "x_lo", "core", "x_hi")
PARAMS_ALL = 3932160
FREQ_FIRST = 9
PLANE_FIRST = 19
Z_FIRST = 9
SPLITS = 3


def sens_kernel(
    ids,
    mass_in,
    weights_in,
    fwd,
    adj,
    size,
    out,
    mass,
    weights,
    e_buf,
    l_buf,
    scale_buf,
    mixed,
    e_sem,
    l_sem,
    small_sem,
):
    rows = PER_STEP * ROWS
    steps = GROUPS // PER_STEP
    small = [
        pltpu.make_async_copy(mass_in, mass, small_sem.at[0]),
        pltpu.make_async_copy(weights_in, weights, small_sem.at[1]),
        pltpu.make_async_copy(size, scale_buf, small_sem.at[2]),
    ]

    def copies(i):
        span = pl.ds(pl.multiple_of(i * 2 * rows, 2 * rows), 2 * rows)
        return (
            pltpu.make_async_copy(fwd.at[:, span, :], e_buf.at[:, span, :], e_sem.at[i]),
            pltpu.make_async_copy(adj.at[:, span, :], l_buf.at[:, span, :], l_sem.at[i]),
        )

    for copy in small:
        copy.start()
    for i in range(steps):
        for copy in copies(i):
            copy.start()
    for copy in small:
        copy.wait()
    weight = weights[ids[0]]

    @pl.loop(0, steps)
    def _(i):
        for copy in copies(i):
            copy.wait()
        scale = scale_buf[pl.ds(pl.multiple_of(i * rows, 8), rows), :] * weight
        for k in range(3):
            for first in range(0, 2 * rows, 16):
                span = pl.ds(pl.multiple_of(i * 2 * rows + first, 16), 16)
                e = [e_buf[4 * k + b, span, :].astype(jnp.float32) for b in range(4)]
                total = None
                for a in range(4):
                    coupled = mass[k, a, 0] * e[0]
                    for b in range(1, 4):
                        coupled = coupled + mass[k, a, b] * e[b]
                    term = l_buf[4 * k + a, span, :].astype(jnp.float32) * coupled
                    total = term if total is None else total + term
                mixed[k, first : first + 16, :] = total
        for k in range(3):
            sens = mixed[k, pl.ds(0, rows, stride=2), :] - mixed[k, pl.ds(1, rows, stride=2), :]
            sens = sens * scale
            for owner in range(PER_STEP):
                out[(i ^ FREQ_FIRST // PER_STEP) * PER_STEP + (owner ^ FREQ_FIRST % PER_STEP), k * ROWS : (k + 1) * ROWS, :] = sens[owner * ROWS : (owner + 1) * ROWS, :]


def sens_to_owners(fwd, adj, mass, size, weights, ids):
    smem = pl.BlockSpec(memory_space=pltpu.SMEM)
    hbm = pl.BlockSpec(memory_space=pltpu.HBM)
    rows = PER_STEP * ROWS
    steps = GROUPS // PER_STEP
    return pl.pallas_call(
        sens_kernel,
        out_shape=jax.ShapeDtypeStruct((GROUPS, PACK, LANES), jnp.float32),
        in_specs=[smem, hbm, hbm, hbm, hbm, hbm],
        out_specs=pl.BlockSpec(memory_space=pltpu.VMEM),
        scratch_shapes=[
            pltpu.SMEM(mass.shape, mass.dtype),
            pltpu.SMEM(weights.shape, weights.dtype),
            pltpu.VMEM(fwd.shape, fwd.dtype),
            pltpu.VMEM(adj.shape, adj.dtype),
            pltpu.VMEM(size.shape, size.dtype),
            pltpu.VMEM((3, 2 * rows, LANES), jnp.float32),
            pltpu.SemaphoreType.DMA((steps,)),
            pltpu.SemaphoreType.DMA((steps,)),
            pltpu.SemaphoreType.DMA((3,)),
        ],
        compiler_params=pltpu.CompilerParams(vmem_limit_bytes=12 << 20),
        name="sens",
    )(ids, *[pltpu.with_memory_space_constraint(each, pltpu.HBM) for each in (mass, weights, fwd, adj, size)])


def split(values):
    parts = []
    for _ in range(SPLITS):
        parts.append(values.astype(jnp.bfloat16))
        values = values - parts[-1].astype(jnp.float32)
    return parts


def products_kernel(
    cells, sens, steps, grads, gradient_out, precond, out, gradient, total_rows, damped_rows, gradient_sem
):
    owner = lax.axis_index(("x_hi", "z")) * GROUPS + lax.axis_index(FREQ)
    offset = cells[...] - owner * (ROWS * LANES)
    inside = (offset >= 0) & (offset < ROWS * LANES)
    row = jnp.where(inside, offset >> 7, -1)
    lane = offset & (LANES - 1)
    place = lax.broadcasted_iota(jnp.int32, (PACK, LANES), 0)
    place = jnp.where(place < 2 * ROWS, jnp.where(place < ROWS, place, place - ROWS), place - 2 * ROWS)
    column = lax.broadcasted_iota(jnp.int32, (LANES, LANES), 0)
    row_hot, lane_hot = [], []
    for q in range(8):
        row_hot.append((row[q : q + 1, :] == place).astype(jnp.float32).astype(jnp.bfloat16))
        lane_hot.append((lane[q : q + 1, :] == column).astype(jnp.float32).astype(jnp.bfloat16))
    hits = lax.dot_general(
        jnp.concatenate(row_hot, axis=1),
        jnp.concatenate(lane_hot, axis=1),
        (((1,), (1,)), ((), ())),
        preferred_element_type=jnp.float32,
    )
    total = sens[0:PACK, :]
    for f in range(1, SLOTS):
        total = total + sens[f * PACK : (f + 1) * PACK, :]
    total_rows[...] = total
    for r in range(ROWS):
        gradient[:, r * LANES : (r + 1) * LANES] = total_rows[pl.ds(r, 3, stride=ROWS), :]
    gradient_copy = pltpu.make_async_copy(gradient, gradient_out, gradient_sem)
    gradient_copy.start()
    damped_rows[...] = total / (1.0 + 4.0 * hits)
    for r in range(ROWS):
        precond[:, r * LANES : (r + 1) * LANES] = damped_rows[pl.ds(r, 3, stride=ROWS), :]
    products = jnp.zeros((144, 144), jnp.float32)
    for k in range(3):
        slots, damped = [], []
        for r in range(ROWS):
            slots.append(sens[pl.ds(k * ROWS + r, SLOTS, stride=PACK), :])
            damped.append(jnp.broadcast_to(damped_rows[k * ROWS + r : k * ROWS + r + 1, :], (16, LANES)))
        pairs = split(jnp.concatenate([steps[k], grads[k]], axis=0))
        slots = split(jnp.concatenate(slots, axis=1))
        damped = split(jnp.concatenate(damped, axis=1))
        products = products + lax.dot_general(
            jnp.concatenate([*pairs, *slots], axis=0),
            jnp.concatenate([*pairs, *damped], axis=0),
            (((1,), (1,)), ((), ())),
            preferred_element_type=jnp.float32,
        )
    products = sum(
        products[:, 32 * b : 32 * b + 32] for b in reversed(range(SPLITS))
    ), sum(products[:, 32 * SPLITS + 16 * b : 32 * SPLITS + 16 * b + 16] for b in reversed(range(SPLITS)))
    products = jnp.concatenate(products, axis=1)
    products = jnp.concatenate(
        [
            sum(products[32 * a : 32 * a + 32] for a in reversed(range(SPLITS))),
            sum(products[32 * SPLITS + 16 * a : 32 * SPLITS + 16 * a + 16] for a in reversed(range(SPLITS))),
        ],
        axis=0,
    )
    s, y, f = products[:16], products[16:32], products[32:]
    row = lax.broadcasted_iota(jnp.int32, (16, 16), 0)
    lane = lax.broadcasted_iota(jnp.int32, (16, 16), 1)
    grad_gram = y[:, 16:32]
    block = jnp.concatenate(
        [
            jnp.where(row <= lane, s[:, 16:32], grad_gram),
            jnp.sum(jnp.where(row == lane, grad_gram, 0.0), axis=1, keepdims=True),
            f[:, 0:32],
            s[:, 32:33],
            y[:, 32:33],
            f[:, 32:33],
            jnp.zeros((16, 12), jnp.float32),
        ],
        axis=1,
    )
    block = jnp.concatenate([block[:8], block[8:]], axis=1)
    for i in range(out.shape[0]):
        out[i] = block
    gradient_copy.wait()


def inner_products(cells, sens, steps, grads, copies):
    vmem = pl.BlockSpec(memory_space=pltpu.VMEM)
    own = jax.ShapeDtypeStruct((3, ROWS * LANES), jnp.float32)
    return pl.pallas_call(
        products_kernel,
        out_shape=(own, own, jax.ShapeDtypeStruct((copies, 8, LANES), jnp.float32)),
        in_specs=[vmem] * 4,
        out_specs=(pl.BlockSpec(memory_space=pltpu.HBM), vmem, vmem),
        scratch_shapes=[
            pltpu.VMEM(own.shape, own.dtype),
            pltpu.VMEM((PACK, LANES), jnp.float32),
            pltpu.VMEM((PACK, LANES), jnp.float32),
            pltpu.SemaphoreType.DMA(()),
        ],
        compiler_params=pltpu.CompilerParams(vmem_limit_bytes=12 << 20),
        name="products",
    )(cells, sens, steps, grads)


def resend_kernel(parts, out):
    total = jnp.sum(parts[...], axis=0)
    for i in range(out.shape[0]):
        out[i] = total


def resend(parts, copies):
    vmem = pl.BlockSpec(memory_space=pltpu.VMEM)
    return pl.pallas_call(
        resend_kernel,
        out_shape=jax.ShapeDtypeStruct((copies, 8, LANES), jnp.float32),
        in_specs=[vmem],
        out_specs=vmem,
        compiler_params=pltpu.CompilerParams(vmem_limit_bytes=4 << 20),
        name="resend",
    )(parts)


def direction_kernel(parts, steps, grads, precond, direction, predicted):
    halves = jnp.sum(parts[...], axis=0)
    block = jnp.concatenate([halves[:, :64], halves[:, 64:]], axis=0)
    turned = jnp.concatenate([block, jnp.zeros((16, 64), jnp.float32)], axis=1)
    turned = jnp.concatenate([turned, jnp.zeros((LANES - 16, LANES), jnp.float32)], axis=0).T[:16]
    row = lax.broadcasted_iota(jnp.int32, (16, LANES), 0)
    lane = lax.broadcasted_iota(jnp.int32, (16, LANES), 1)

    def column(i, of=block):
        return jnp.broadcast_to(of[:, i : i + 1], (16, LANES))

    def place(i, value, into):
        return jnp.where(row == i, jnp.broadcast_to(value, (16, LANES)), into)

    diagonal = jnp.where(row[:, :64] == lane[:, :64], block, 0.0)
    diagonal = jnp.broadcast_to(jnp.sum(diagonal, axis=1, keepdims=True), (16, LANES))
    grad_diagonal = column(16)
    gamma = jnp.broadcast_to(diagonal[15:16, :] / grad_diagonal[15:16, :], (16, LANES))
    rest = column(49)
    first = jnp.zeros((16, LANES), jnp.float32)
    along = jnp.zeros((16, LANES), jnp.float32)
    slots_first = jnp.zeros((16, LANES), jnp.float32)
    for m in range(15, -1, -1):
        value = rest[m : m + 1, :] / diagonal[m : m + 1, :]
        upper = column(m)
        rest = rest - upper * value
        grad_column = jnp.where(row > m, upper, jnp.where(row < m, column(m, turned), grad_diagonal))
        along = along + grad_column * value
        slots_first = slots_first + column(33 + m) * value
        first = place(m, value, first)
    rest = diagonal * first + gamma * along - gamma * column(50)
    second = jnp.zeros((16, LANES), jnp.float32)
    slots_second = jnp.zeros((16, LANES), jnp.float32)
    for m in range(16):
        value = rest[m : m + 1, :] / diagonal[m : m + 1, :]
        rest = rest - column(m, turned) * value
        slots_second = slots_second + column(17 + m) * value
        second = place(m, value, second)
    change = -(gamma * column(51) + slots_second - gamma * slots_first) / PARAMS_ALL
    predicted[...] = jnp.sum(jnp.where(row == (lane ^ FREQ_FIRST), change, 0.0), axis=0)[:SLOTS]
    scaled = gamma * first
    for k in range(3):
        for r in range(ROWS):
            span = slice(r * LANES, (r + 1) * LANES)
            terms = second * steps[k, :, span] - scaled * grads[k, :, span]
            total = jnp.sum(terms, axis=0, keepdims=True)
            direction[k : k + 1, span] = -(gamma[0:1, :] * precond[k : k + 1, span] + total)


def directions(parts, steps, grads, precond):
    vmem = pl.BlockSpec(memory_space=pltpu.VMEM)
    own = jax.ShapeDtypeStruct((3, ROWS * LANES), jnp.float32)
    return pl.pallas_call(
        direction_kernel,
        out_shape=(own, jax.ShapeDtypeStruct((SLOTS,), jnp.float32)),
        in_specs=[vmem] * 4,
        out_specs=(vmem, vmem),
        compiler_params=pltpu.CompilerParams(vmem_limit_bytes=8 << 20),
        name="direction",
    )(parts, steps, grads, precond)


def field_rows(field):
    split = field.reshape(2, EDGES, SLAB_ROWS, LANES)
    return split.transpose(1, 2, 0, 3).reshape(EDGES, 2 * SLAB_ROWS, LANES)


def listed(count, first):
    return [[(i + first) % count for i in range(count)]]


def local(
    forward_field,
    adjoint_field,
    mass_block,
    cell_size,
    freq_weight,
    freq_ids,
    receiver_cells,
    step_pairs,
    grad_pairs,
):
    steps = step_pairs.transpose(1, 0, 2)
    grads = grad_pairs.transpose(1, 0, 2)
    packed = sens_to_owners(
        field_rows(forward_field),
        field_rows(adjoint_field),
        mass_block,
        cell_size.reshape(SLAB_ROWS, LANES),
        freq_weight,
        freq_ids,
    )
    arrived = lax.all_to_all(packed, FREQ, 0, 0, tiled=True, axis_index_groups=[[i ^ FREQ_FIRST for i in range(16)]])
    gradient, precond, block = inner_products(
        receiver_cells.reshape(8, LANES),
        arrived.reshape(SLOTS * PACK, LANES),
        steps,
        grads,
        lax.axis_size(PLANE),
    )
    parts = lax.all_to_all(block, PLANE, 0, 0, tiled=True, axis_index_groups=listed(32, PLANE_FIRST))
    parts = lax.all_to_all(resend(parts, lax.axis_size("z")), "z", 0, 0, tiled=True, axis_index_groups=listed(16, Z_FIRST))
    direction, predicted = directions(parts, steps, grads, precond)
    return (gradient, direction, predicted)


def solution(mesh):
    axes = ("y", "x_lo", "core", "x_hi", "z")
    parts = jax.sharding.Mesh(mesh.devices.reshape(4, 2, 2, 2, 16), axes)
    slab = ("x_hi", "z")
    owned = P(None, None, slab + FREQ)
    in_specs = (
        P(FREQ, None, None, slab),
        P(FREQ, None, None, slab),
        P(),
        P(slab),
        P(),
        P(FREQ),
        P(),
        owned,
        owned,
    )
    out_specs = (P(None, slab + FREQ), P(None, slab + FREQ), P())
    return jax.shard_map(local, mesh=parts, in_specs=in_specs, out_specs=out_specs, check_vma=False)
```

```python
import jax
import jax.numpy as jnp
from jax import lax
from jax.experimental import pallas as pl
from jax.experimental.pallas import tpu as pltpu
from jax.sharding import PartitionSpec as P

LANES = 128
PAIRS = 16
SLOTS = 16
EDGES = 12
GROUPS = 16
ROWS = 20
SLAB_ROWS = GROUPS * ROWS
PACK = 64
PER_STEP = 4
FREQ = ("y", "x_lo", "core")
PLANE = ("y", "x_lo", "core", "x_hi")
PARAMS_ALL = 3932160
FREQ_FIRST = 9
PLANE_FIRST = 19
Z_FIRST = 9
SPLITS = 3


def own_divisor(cells):
    owner = lax.axis_index(("x_hi", "z")) * GROUPS + lax.axis_index(FREQ)
    offset = cells - owner * (ROWS * LANES)
    inside = (offset >= 0) & (offset < ROWS * LANES)
    row = jnp.where(inside, offset >> 7, -1)
    lane = offset & (LANES - 1)
    place = lax.broadcasted_iota(jnp.int32, (PACK, LANES), 0)
    place = jnp.where(place < 2 * ROWS, jnp.where(place < ROWS, place, place - ROWS), place - 2 * ROWS)
    column = lax.broadcasted_iota(jnp.int32, (LANES, LANES), 0)
    row_hot, lane_hot = [], []
    for q in range(8):
        row_hot.append((row[q : q + 1, :] == place).astype(jnp.float32).astype(jnp.bfloat16))
        lane_hot.append((lane[q : q + 1, :] == column).astype(jnp.float32).astype(jnp.bfloat16))
    return 1.0 + 4.0 * lax.dot_general(
        jnp.concatenate(row_hot, axis=1),
        jnp.concatenate(lane_hot, axis=1),
        (((1,), (1,)), ((), ())),
        preferred_element_type=jnp.float32,
    )


def sens_kernel(
    ids,
    mass_in,
    weights_in,
    cells_in,
    fwd,
    adj,
    size,
    out,
    divisor,
    mass,
    weights,
    cells,
    e_buf,
    l_buf,
    scale_buf,
    mixed,
    e_sem,
    l_sem,
    small_sem,
):
    rows = PER_STEP * ROWS
    steps = GROUPS // PER_STEP
    small = [
        pltpu.make_async_copy(cells_in, cells, small_sem.at[3]),
        pltpu.make_async_copy(mass_in, mass, small_sem.at[0]),
        pltpu.make_async_copy(weights_in, weights, small_sem.at[1]),
        pltpu.make_async_copy(size, scale_buf, small_sem.at[2]),
    ]

    def copies(i):
        span = pl.ds(pl.multiple_of(i * 2 * rows, 2 * rows), 2 * rows)
        return (
            pltpu.make_async_copy(fwd.at[:, span, :], e_buf.at[:, span, :], e_sem.at[i]),
            pltpu.make_async_copy(adj.at[:, span, :], l_buf.at[:, span, :], l_sem.at[i]),
        )

    for copy in small:
        copy.start()
    for i in range(steps):
        for copy in copies(i):
            copy.start()
    small[0].wait()
    divisor[...] = own_divisor(cells[...])
    for copy in small[1:]:
        copy.wait()
    weight = weights[ids[0]]

    @pl.loop(0, steps)
    def _(i):
        for copy in copies(i):
            copy.wait()
        scale = scale_buf[pl.ds(pl.multiple_of(i * rows, 8), rows), :] * weight
        for k in range(3):
            for first in range(0, 2 * rows, 16):
                span = pl.ds(pl.multiple_of(i * 2 * rows + first, 16), 16)
                e = [e_buf[4 * k + b, span, :].astype(jnp.float32) for b in range(4)]
                total = None
                for a in range(4):
                    coupled = mass[k, a, 0] * e[0]
                    for b in range(1, 4):
                        coupled = coupled + mass[k, a, b] * e[b]
                    term = l_buf[4 * k + a, span, :].astype(jnp.float32) * coupled
                    total = term if total is None else total + term
                mixed[k, first : first + 16, :] = total
        for k in range(3):
            sens = mixed[k, pl.ds(0, rows, stride=2), :] - mixed[k, pl.ds(1, rows, stride=2), :]
            sens = sens * scale
            for owner in range(PER_STEP):
                out[(i ^ FREQ_FIRST // PER_STEP) * PER_STEP + (owner ^ FREQ_FIRST % PER_STEP), k * ROWS : (k + 1) * ROWS, :] = sens[owner * ROWS : (owner + 1) * ROWS, :]


def sens_to_owners(fwd, adj, mass, size, weights, ids, cells):
    smem = pl.BlockSpec(memory_space=pltpu.SMEM)
    hbm = pl.BlockSpec(memory_space=pltpu.HBM)
    rows = PER_STEP * ROWS
    steps = GROUPS // PER_STEP
    return pl.pallas_call(
        sens_kernel,
        out_shape=(
            jax.ShapeDtypeStruct((GROUPS, PACK, LANES), jnp.float32),
            jax.ShapeDtypeStruct((PACK, LANES), jnp.float32),
        ),
        in_specs=[smem, hbm, hbm, hbm, hbm, hbm, hbm],
        out_specs=(pl.BlockSpec(memory_space=pltpu.VMEM),) * 2,
        scratch_shapes=[
            pltpu.SMEM(mass.shape, mass.dtype),
            pltpu.SMEM(weights.shape, weights.dtype),
            pltpu.VMEM(cells.shape, cells.dtype),
            pltpu.VMEM(fwd.shape, fwd.dtype),
            pltpu.VMEM(adj.shape, adj.dtype),
            pltpu.VMEM(size.shape, size.dtype),
            pltpu.VMEM((3, 2 * rows, LANES), jnp.float32),
            pltpu.SemaphoreType.DMA((steps,)),
            pltpu.SemaphoreType.DMA((steps,)),
            pltpu.SemaphoreType.DMA((4,)),
        ],
        compiler_params=pltpu.CompilerParams(vmem_limit_bytes=12 << 20),
        name="sens",
    )(ids, *[pltpu.with_memory_space_constraint(each, pltpu.HBM) for each in (mass, weights, cells, fwd, adj, size)])


def split(values):
    parts = []
    for _ in range(SPLITS):
        parts.append(values.astype(jnp.bfloat16))
        values = values - parts[-1].astype(jnp.float32)
    return parts


def products_kernel(
    divisor, sens, steps, grads, gradient_out, precond, out, gradient, total_rows, damped_rows, gradient_sem
):
    total = sens[0:PACK, :]
    for f in range(1, SLOTS):
        total = total + sens[f * PACK : (f + 1) * PACK, :]
    total_rows[...] = total
    for r in range(ROWS):
        gradient[:, r * LANES : (r + 1) * LANES] = total_rows[pl.ds(r, 3, stride=ROWS), :]
    gradient_copy = pltpu.make_async_copy(gradient, gradient_out, gradient_sem)
    gradient_copy.start()
    damped_rows[...] = total / divisor[...]
    for r in range(ROWS):
        precond[:, r * LANES : (r + 1) * LANES] = damped_rows[pl.ds(r, 3, stride=ROWS), :]
    products = jnp.zeros((144, 144), jnp.float32)
    for k in range(3):
        slots, damped = [], []
        for r in range(ROWS):
            slots.append(sens[pl.ds(k * ROWS + r, SLOTS, stride=PACK), :])
            damped.append(jnp.broadcast_to(damped_rows[k * ROWS + r : k * ROWS + r + 1, :], (16, LANES)))
        pairs = split(jnp.concatenate([steps[k], grads[k]], axis=0))
        slots = split(jnp.concatenate(slots, axis=1))
        damped = split(jnp.concatenate(damped, axis=1))
        products = products + lax.dot_general(
            jnp.concatenate([*pairs, *slots], axis=0),
            jnp.concatenate([*pairs, *damped], axis=0),
            (((1,), (1,)), ((), ())),
            preferred_element_type=jnp.float32,
        )
    products = sum(
        products[:, 32 * b : 32 * b + 32] for b in reversed(range(SPLITS))
    ), sum(products[:, 32 * SPLITS + 16 * b : 32 * SPLITS + 16 * b + 16] for b in reversed(range(SPLITS)))
    products = jnp.concatenate(products, axis=1)
    products = jnp.concatenate(
        [
            sum(products[32 * a : 32 * a + 32] for a in reversed(range(SPLITS))),
            sum(products[32 * SPLITS + 16 * a : 32 * SPLITS + 16 * a + 16] for a in reversed(range(SPLITS))),
        ],
        axis=0,
    )
    s, y, f = products[:16], products[16:32], products[32:]
    row = lax.broadcasted_iota(jnp.int32, (16, 16), 0)
    lane = lax.broadcasted_iota(jnp.int32, (16, 16), 1)
    grad_gram = y[:, 16:32]
    block = jnp.concatenate(
        [
            jnp.where(row <= lane, s[:, 16:32], grad_gram),
            jnp.sum(jnp.where(row == lane, grad_gram, 0.0), axis=1, keepdims=True),
            f[:, 0:32],
            s[:, 32:33],
            y[:, 32:33],
            f[:, 32:33],
            jnp.zeros((16, 12), jnp.float32),
        ],
        axis=1,
    )
    block = jnp.concatenate([block[:8], block[8:]], axis=1)
    for i in range(out.shape[0]):
        out[i] = block
    gradient_copy.wait()


def inner_products(divisor, sens, steps, grads, copies):
    vmem = pl.BlockSpec(memory_space=pltpu.VMEM)
    own = jax.ShapeDtypeStruct((3, ROWS * LANES), jnp.float32)
    return pl.pallas_call(
        products_kernel,
        out_shape=(own, own, jax.ShapeDtypeStruct((copies, 8, LANES), jnp.float32)),
        in_specs=[vmem] * 4,
        out_specs=(pl.BlockSpec(memory_space=pltpu.HBM), vmem, vmem),
        scratch_shapes=[
            pltpu.VMEM(own.shape, own.dtype),
            pltpu.VMEM((PACK, LANES), jnp.float32),
            pltpu.VMEM((PACK, LANES), jnp.float32),
            pltpu.SemaphoreType.DMA(()),
        ],
        compiler_params=pltpu.CompilerParams(vmem_limit_bytes=12 << 20),
        name="products",
    )(divisor, sens, steps, grads)


def resend_kernel(parts, out):
    total = jnp.sum(parts[...], axis=0)
    for i in range(out.shape[0]):
        out[i] = total


def resend(parts, copies):
    vmem = pl.BlockSpec(memory_space=pltpu.VMEM)
    return pl.pallas_call(
        resend_kernel,
        out_shape=jax.ShapeDtypeStruct((copies, 8, LANES), jnp.float32),
        in_specs=[vmem],
        out_specs=vmem,
        compiler_params=pltpu.CompilerParams(vmem_limit_bytes=4 << 20),
        name="resend",
    )(parts)


def direction_kernel(parts, steps, grads, precond, direction, predicted):
    halves = jnp.sum(parts[...], axis=0)
    block = jnp.concatenate([halves[:, :64], halves[:, 64:]], axis=0)
    turned = jnp.concatenate([block, jnp.zeros((16, 64), jnp.float32)], axis=1)
    turned = jnp.concatenate([turned, jnp.zeros((LANES - 16, LANES), jnp.float32)], axis=0).T[:16]
    row = lax.broadcasted_iota(jnp.int32, (16, LANES), 0)
    lane = lax.broadcasted_iota(jnp.int32, (16, LANES), 1)

    def column(i, of=block):
        return jnp.broadcast_to(of[:, i : i + 1], (16, LANES))

    def place(i, value, into):
        return jnp.where(row == i, jnp.broadcast_to(value, (16, LANES)), into)

    diagonal = jnp.where(row[:, :64] == lane[:, :64], block, 0.0)
    diagonal = jnp.broadcast_to(jnp.sum(diagonal, axis=1, keepdims=True), (16, LANES))
    grad_diagonal = column(16)
    gamma = jnp.broadcast_to(diagonal[15:16, :] / grad_diagonal[15:16, :], (16, LANES))
    rest = column(49)
    first = jnp.zeros((16, LANES), jnp.float32)
    along = jnp.zeros((16, LANES), jnp.float32)
    slots_first = jnp.zeros((16, LANES), jnp.float32)
    for m in range(15, -1, -1):
        value = rest[m : m + 1, :] / diagonal[m : m + 1, :]
        upper = column(m)
        rest = rest - upper * value
        grad_column = jnp.where(row > m, upper, jnp.where(row < m, column(m, turned), grad_diagonal))
        along = along + grad_column * value
        slots_first = slots_first + column(33 + m) * value
        first = place(m, value, first)
    rest = diagonal * first + gamma * along - gamma * column(50)
    second = jnp.zeros((16, LANES), jnp.float32)
    slots_second = jnp.zeros((16, LANES), jnp.float32)
    for m in range(16):
        value = rest[m : m + 1, :] / diagonal[m : m + 1, :]
        rest = rest - column(m, turned) * value
        slots_second = slots_second + column(17 + m) * value
        second = place(m, value, second)
    change = -(gamma * column(51) + slots_second - gamma * slots_first) / PARAMS_ALL
    predicted[...] = jnp.sum(jnp.where(row == (lane ^ FREQ_FIRST), change, 0.0), axis=0)[:SLOTS]
    scaled = gamma * first
    for k in range(3):
        for r in range(ROWS):
            span = slice(r * LANES, (r + 1) * LANES)
            terms = second * steps[k, :, span] - scaled * grads[k, :, span]
            total = jnp.sum(terms, axis=0, keepdims=True)
            direction[k : k + 1, span] = -(gamma[0:1, :] * precond[k : k + 1, span] + total)


def directions(parts, steps, grads, precond):
    vmem = pl.BlockSpec(memory_space=pltpu.VMEM)
    own = jax.ShapeDtypeStruct((3, ROWS * LANES), jnp.float32)
    return pl.pallas_call(
        direction_kernel,
        out_shape=(own, jax.ShapeDtypeStruct((SLOTS,), jnp.float32)),
        in_specs=[vmem] * 4,
        out_specs=(vmem, vmem),
        compiler_params=pltpu.CompilerParams(vmem_limit_bytes=8 << 20),
        name="direction",
    )(parts, steps, grads, precond)


def field_rows(field):
    split = field.reshape(2, EDGES, SLAB_ROWS, LANES)
    return split.transpose(1, 2, 0, 3).reshape(EDGES, 2 * SLAB_ROWS, LANES)


def listed(count, first):
    return [[(i + first) % count for i in range(count)]]


def local(
    forward_field,
    adjoint_field,
    mass_block,
    cell_size,
    freq_weight,
    freq_ids,
    receiver_cells,
    step_pairs,
    grad_pairs,
):
    steps = step_pairs.transpose(1, 0, 2)
    grads = grad_pairs.transpose(1, 0, 2)
    packed, divisor = sens_to_owners(
        field_rows(forward_field),
        field_rows(adjoint_field),
        mass_block,
        cell_size.reshape(SLAB_ROWS, LANES),
        freq_weight,
        freq_ids,
        receiver_cells.reshape(8, LANES),
    )
    arrived = lax.all_to_all(packed, FREQ, 0, 0, tiled=True, axis_index_groups=[[i ^ FREQ_FIRST for i in range(16)]])
    gradient, precond, block = inner_products(
        divisor,
        arrived.reshape(SLOTS * PACK, LANES),
        steps,
        grads,
        lax.axis_size(PLANE),
    )
    parts = lax.all_to_all(block, PLANE, 0, 0, tiled=True, axis_index_groups=listed(32, PLANE_FIRST))
    parts = lax.all_to_all(resend(parts, lax.axis_size("z")), "z", 0, 0, tiled=True, axis_index_groups=listed(16, Z_FIRST))
    direction, predicted = directions(parts, steps, grads, precond)
    return (gradient, direction, predicted)


def solution(mesh):
    axes = ("y", "x_lo", "core", "x_hi", "z")
    parts = jax.sharding.Mesh(mesh.devices.reshape(4, 2, 2, 2, 16), axes)
    slab = ("x_hi", "z")
    owned = P(None, None, slab + FREQ)
    in_specs = (
        P(FREQ, None, None, slab),
        P(FREQ, None, None, slab),
        P(),
        P(slab),
        P(),
        P(FREQ),
        P(),
        owned,
        owned,
    )
    out_specs = (P(None, slab + FREQ), P(None, slab + FREQ), P())
    return jax.shard_map(local, mesh=parts, in_specs=in_specs, out_specs=out_specs, check_vma=False)
```

```python
import jax
import jax.numpy as jnp
from jax import lax
from jax.experimental import pallas as pl
from jax.experimental.pallas import tpu as pltpu
from jax.sharding import PartitionSpec as P

LANES = 128
PAIRS = 16
SLOTS = 16
EDGES = 12
GROUPS = 16
ROWS = 20
SLAB_ROWS = GROUPS * ROWS
PACK = 64
PER_STEP = 4
FREQ = ("y", "x_lo", "core")
PLANE = ("y", "x_lo", "core", "x_hi")
PARAMS_ALL = 3932160
FREQ_FIRST = 9
PLANE_FIRST = 19
Z_FIRST = 9
SPLITS = 3


def own_divisor(cells):
    owner = lax.axis_index(("x_hi", "z")) * GROUPS + lax.axis_index(FREQ)
    offset = cells - owner * (ROWS * LANES)
    inside = (offset >= 0) & (offset < ROWS * LANES)
    row = jnp.where(inside, offset >> 7, -1)
    lane = offset & (LANES - 1)
    place = lax.broadcasted_iota(jnp.int32, (PACK, LANES), 0)
    place = jnp.where(place < 2 * ROWS, jnp.where(place < ROWS, place, place - ROWS), place - 2 * ROWS)
    column = lax.broadcasted_iota(jnp.int32, (LANES, LANES), 0)
    row_hot, lane_hot = [], []
    for q in range(8):
        row_hot.append((row[q : q + 1, :] == place).astype(jnp.float32).astype(jnp.bfloat16))
        lane_hot.append((lane[q : q + 1, :] == column).astype(jnp.float32).astype(jnp.bfloat16))
    return 1.0 + 4.0 * lax.dot_general(
        jnp.concatenate(row_hot, axis=1),
        jnp.concatenate(lane_hot, axis=1),
        (((1,), (1,)), ((), ())),
        preferred_element_type=jnp.float32,
    )


def sens_kernel(
    ids,
    mass_in,
    weights_in,
    cells_in,
    fwd,
    adj,
    size,
    out,
    divisor,
    mass,
    weights,
    cells,
    e_buf,
    l_buf,
    scale_buf,
    mixed,
    e_sem,
    l_sem,
    small_sem,
):
    rows = PER_STEP * ROWS
    steps = GROUPS // PER_STEP
    small = [
        pltpu.make_async_copy(cells_in, cells, small_sem.at[3]),
        pltpu.make_async_copy(mass_in, mass, small_sem.at[0]),
        pltpu.make_async_copy(weights_in, weights, small_sem.at[1]),
        pltpu.make_async_copy(size, scale_buf, small_sem.at[2]),
    ]

    def copies(i):
        span = pl.ds(pl.multiple_of(i * 2 * rows, 2 * rows), 2 * rows)
        return (
            pltpu.make_async_copy(fwd.at[:, span, :], e_buf.at[:, span, :], e_sem.at[i]),
            pltpu.make_async_copy(adj.at[:, span, :], l_buf.at[:, span, :], l_sem.at[i]),
        )

    for copy in small:
        copy.start()
    for i in range(steps):
        for copy in copies(i):
            copy.start()
    small[0].wait()
    divisor[...] = own_divisor(cells[...])
    for copy in small[1:]:
        copy.wait()
    weight = weights[ids[0]]

    @pl.loop(0, steps)
    def _(i):
        for copy in copies(i):
            copy.wait()
        scale = scale_buf[pl.ds(pl.multiple_of(i * rows, 8), rows), :] * weight
        for k in range(3):
            factor = [[jnp.full((16, LANES), mass[k, a, b]) for b in range(4)] for a in range(4)]
            for first in range(0, 2 * rows, 16):
                span = pl.ds(pl.multiple_of(i * 2 * rows + first, 16), 16)
                e = [e_buf[4 * k + b, span, :].astype(jnp.float32) for b in range(4)]
                total = None
                for a in range(4):
                    coupled = factor[a][0] * e[0]
                    for b in range(1, 4):
                        coupled = coupled + factor[a][b] * e[b]
                    term = l_buf[4 * k + a, span, :].astype(jnp.float32) * coupled
                    total = term if total is None else total + term
                mixed[k, first : first + 16, :] = total
        for k in range(3):
            sens = mixed[k, pl.ds(0, rows, stride=2), :] - mixed[k, pl.ds(1, rows, stride=2), :]
            sens = sens * scale
            for owner in range(PER_STEP):
                out[(i ^ FREQ_FIRST // PER_STEP) * PER_STEP + (owner ^ FREQ_FIRST % PER_STEP), k * ROWS : (k + 1) * ROWS, :] = sens[owner * ROWS : (owner + 1) * ROWS, :]


def sens_to_owners(fwd, adj, mass, size, weights, ids, cells):
    smem = pl.BlockSpec(memory_space=pltpu.SMEM)
    hbm = pl.BlockSpec(memory_space=pltpu.HBM)
    rows = PER_STEP * ROWS
    steps = GROUPS // PER_STEP
    return pl.pallas_call(
        sens_kernel,
        out_shape=(
            jax.ShapeDtypeStruct((GROUPS, PACK, LANES), jnp.float32),
            jax.ShapeDtypeStruct((PACK, LANES), jnp.float32),
        ),
        in_specs=[smem, hbm, hbm, hbm, hbm, hbm, hbm],
        out_specs=(pl.BlockSpec(memory_space=pltpu.VMEM),) * 2,
        scratch_shapes=[
            pltpu.SMEM(mass.shape, mass.dtype),
            pltpu.SMEM(weights.shape, weights.dtype),
            pltpu.VMEM(cells.shape, cells.dtype),
            pltpu.VMEM(fwd.shape, fwd.dtype),
            pltpu.VMEM(adj.shape, adj.dtype),
            pltpu.VMEM(size.shape, size.dtype),
            pltpu.VMEM((3, 2 * rows, LANES), jnp.float32),
            pltpu.SemaphoreType.DMA((steps,)),
            pltpu.SemaphoreType.DMA((steps,)),
            pltpu.SemaphoreType.DMA((4,)),
        ],
        compiler_params=pltpu.CompilerParams(vmem_limit_bytes=12 << 20),
        name="sens",
    )(ids, *[pltpu.with_memory_space_constraint(each, pltpu.HBM) for each in (mass, weights, cells, fwd, adj, size)])


def split(values):
    parts = []
    for _ in range(SPLITS):
        parts.append(values.astype(jnp.bfloat16))
        values = values - parts[-1].astype(jnp.float32)
    return parts


def products_kernel(
    divisor, sens, steps, grads, gradient_out, precond, out, gradient, total_rows, damped_rows, gradient_sem
):
    total = sens[0:PACK, :]
    for f in range(1, SLOTS):
        total = total + sens[f * PACK : (f + 1) * PACK, :]
    total_rows[...] = total
    for r in range(ROWS):
        gradient[:, r * LANES : (r + 1) * LANES] = total_rows[pl.ds(r, 3, stride=ROWS), :]
    gradient_copy = pltpu.make_async_copy(gradient, gradient_out, gradient_sem)
    gradient_copy.start()
    damped_rows[...] = total / divisor[...]
    for r in range(ROWS):
        precond[:, r * LANES : (r + 1) * LANES] = damped_rows[pl.ds(r, 3, stride=ROWS), :]
    products = jnp.zeros((144, 144), jnp.float32)
    for k in range(3):
        slots, damped = [], []
        for r in range(ROWS):
            slots.append(sens[pl.ds(k * ROWS + r, SLOTS, stride=PACK), :])
            damped.append(jnp.broadcast_to(damped_rows[k * ROWS + r : k * ROWS + r + 1, :], (16, LANES)))
        pairs = split(jnp.concatenate([steps[k], grads[k]], axis=0))
        slots = split(jnp.concatenate(slots, axis=1))
        damped = split(jnp.concatenate(damped, axis=1))
        products = products + lax.dot_general(
            jnp.concatenate([*pairs, *slots], axis=0),
            jnp.concatenate([*pairs, *damped], axis=0),
            (((1,), (1,)), ((), ())),
            preferred_element_type=jnp.float32,
        )
    products = sum(
        products[:, 32 * b : 32 * b + 32] for b in reversed(range(SPLITS))
    ), sum(products[:, 32 * SPLITS + 16 * b : 32 * SPLITS + 16 * b + 16] for b in reversed(range(SPLITS)))
    products = jnp.concatenate(products, axis=1)
    products = jnp.concatenate(
        [
            sum(products[32 * a : 32 * a + 32] for a in reversed(range(SPLITS))),
            sum(products[32 * SPLITS + 16 * a : 32 * SPLITS + 16 * a + 16] for a in reversed(range(SPLITS))),
        ],
        axis=0,
    )
    s, y, f = products[:16], products[16:32], products[32:]
    row = lax.broadcasted_iota(jnp.int32, (16, 16), 0)
    lane = lax.broadcasted_iota(jnp.int32, (16, 16), 1)
    grad_gram = y[:, 16:32]
    block = jnp.concatenate(
        [
            jnp.where(row <= lane, s[:, 16:32], grad_gram),
            jnp.sum(jnp.where(row == lane, grad_gram, 0.0), axis=1, keepdims=True),
            f[:, 0:32],
            s[:, 32:33],
            y[:, 32:33],
            f[:, 32:33],
            jnp.zeros((16, 12), jnp.float32),
        ],
        axis=1,
    )
    block = jnp.concatenate([block[:8], block[8:]], axis=1)
    for i in range(out.shape[0]):
        out[i] = block
    gradient_copy.wait()


def inner_products(divisor, sens, steps, grads, copies):
    vmem = pl.BlockSpec(memory_space=pltpu.VMEM)
    own = jax.ShapeDtypeStruct((3, ROWS * LANES), jnp.float32)
    return pl.pallas_call(
        products_kernel,
        out_shape=(own, own, jax.ShapeDtypeStruct((copies, 8, LANES), jnp.float32)),
        in_specs=[vmem] * 4,
        out_specs=(pl.BlockSpec(memory_space=pltpu.HBM), vmem, vmem),
        scratch_shapes=[
            pltpu.VMEM(own.shape, own.dtype),
            pltpu.VMEM((PACK, LANES), jnp.float32),
            pltpu.VMEM((PACK, LANES), jnp.float32),
            pltpu.SemaphoreType.DMA(()),
        ],
        compiler_params=pltpu.CompilerParams(vmem_limit_bytes=12 << 20),
        name="products",
    )(divisor, sens, steps, grads)


def resend_kernel(parts, out):
    total = jnp.sum(parts[...], axis=0)
    for i in range(out.shape[0]):
        out[i] = total


def resend(parts, copies):
    vmem = pl.BlockSpec(memory_space=pltpu.VMEM)
    return pl.pallas_call(
        resend_kernel,
        out_shape=jax.ShapeDtypeStruct((copies, 8, LANES), jnp.float32),
        in_specs=[vmem],
        out_specs=vmem,
        compiler_params=pltpu.CompilerParams(vmem_limit_bytes=4 << 20),
        name="resend",
    )(parts)


def direction_kernel(parts, steps, grads, precond, direction, predicted):
    halves = jnp.sum(parts[...], axis=0)
    block = jnp.concatenate([halves[:, :64], halves[:, 64:]], axis=0)
    turned = jnp.concatenate([block, jnp.zeros((16, 64), jnp.float32)], axis=1)
    turned = jnp.concatenate([turned, jnp.zeros((LANES - 16, LANES), jnp.float32)], axis=0).T[:16]
    row = lax.broadcasted_iota(jnp.int32, (16, LANES), 0)
    lane = lax.broadcasted_iota(jnp.int32, (16, LANES), 1)

    def column(i, of=block):
        return jnp.broadcast_to(of[:, i : i + 1], (16, LANES))

    def place(i, value, into):
        return jnp.where(row == i, jnp.broadcast_to(value, (16, LANES)), into)

    diagonal = jnp.where(row[:, :64] == lane[:, :64], block, 0.0)
    diagonal = jnp.broadcast_to(jnp.sum(diagonal, axis=1, keepdims=True), (16, LANES))
    grad_diagonal = column(16)
    gamma = jnp.broadcast_to(diagonal[15:16, :] / grad_diagonal[15:16, :], (16, LANES))
    rest = column(49)
    first = jnp.zeros((16, LANES), jnp.float32)
    along = jnp.zeros((16, LANES), jnp.float32)
    slots_first = jnp.zeros((16, LANES), jnp.float32)
    for m in range(15, -1, -1):
        value = rest[m : m + 1, :] / diagonal[m : m + 1, :]
        upper = column(m)
        rest = rest - upper * value
        grad_column = jnp.where(row > m, upper, jnp.where(row < m, column(m, turned), grad_diagonal))
        along = along + grad_column * value
        slots_first = slots_first + column(33 + m) * value
        first = place(m, value, first)
    rest = diagonal * first + gamma * along - gamma * column(50)
    second = jnp.zeros((16, LANES), jnp.float32)
    slots_second = jnp.zeros((16, LANES), jnp.float32)
    for m in range(16):
        value = rest[m : m + 1, :] / diagonal[m : m + 1, :]
        rest = rest - column(m, turned) * value
        slots_second = slots_second + column(17 + m) * value
        second = place(m, value, second)
    change = -(gamma * column(51) + slots_second - gamma * slots_first) / PARAMS_ALL
    predicted[...] = jnp.sum(jnp.where(row == (lane ^ FREQ_FIRST), change, 0.0), axis=0)[:SLOTS]
    scaled = gamma * first
    for k in range(3):
        for r in range(ROWS):
            span = slice(r * LANES, (r + 1) * LANES)
            terms = second * steps[k, :, span] - scaled * grads[k, :, span]
            total = jnp.sum(terms, axis=0, keepdims=True)
            direction[k : k + 1, span] = -(gamma[0:1, :] * precond[k : k + 1, span] + total)


def directions(parts, steps, grads, precond):
    vmem = pl.BlockSpec(memory_space=pltpu.VMEM)
    own = jax.ShapeDtypeStruct((3, ROWS * LANES), jnp.float32)
    return pl.pallas_call(
        direction_kernel,
        out_shape=(own, jax.ShapeDtypeStruct((SLOTS,), jnp.float32)),
        in_specs=[vmem] * 4,
        out_specs=(vmem, vmem),
        compiler_params=pltpu.CompilerParams(vmem_limit_bytes=8 << 20),
        name="direction",
    )(parts, steps, grads, precond)


def field_rows(field):
    split = field.reshape(2, EDGES, SLAB_ROWS, LANES)
    return split.transpose(1, 2, 0, 3).reshape(EDGES, 2 * SLAB_ROWS, LANES)


def listed(count, first):
    return [[(i + first) % count for i in range(count)]]


def farthest_first(count, first):
    return [[first] + [(first + side * far) % count for far in range(count // 2, 0, -1) for side in (1, -1)][1:]]


def local(
    forward_field,
    adjoint_field,
    mass_block,
    cell_size,
    freq_weight,
    freq_ids,
    receiver_cells,
    step_pairs,
    grad_pairs,
):
    steps = step_pairs.transpose(1, 0, 2)
    grads = grad_pairs.transpose(1, 0, 2)
    packed, divisor = sens_to_owners(
        field_rows(forward_field),
        field_rows(adjoint_field),
        mass_block,
        cell_size.reshape(SLAB_ROWS, LANES),
        freq_weight,
        freq_ids,
        receiver_cells.reshape(8, LANES),
    )
    arrived = lax.all_to_all(packed, FREQ, 0, 0, tiled=True, axis_index_groups=[[i ^ FREQ_FIRST for i in range(16)]])
    gradient, precond, block = inner_products(
        divisor,
        arrived.reshape(SLOTS * PACK, LANES),
        steps,
        grads,
        lax.axis_size(PLANE),
    )
    parts = lax.all_to_all(block, PLANE, 0, 0, tiled=True, axis_index_groups=listed(32, PLANE_FIRST))
    parts = lax.all_to_all(resend(parts, lax.axis_size("z")), "z", 0, 0, tiled=True, axis_index_groups=farthest_first(16, Z_FIRST))
    direction, predicted = directions(parts, steps, grads, precond)
    return (gradient, direction, predicted)


def solution(mesh):
    axes = ("y", "x_lo", "core", "x_hi", "z")
    parts = jax.sharding.Mesh(mesh.devices.reshape(4, 2, 2, 2, 16), axes)
    slab = ("x_hi", "z")
    owned = P(None, None, slab + FREQ)
    in_specs = (
        P(FREQ, None, None, slab),
        P(FREQ, None, None, slab),
        P(),
        P(slab),
        P(),
        P(FREQ),
        P(),
        owned,
        owned,
    )
    out_specs = (P(None, slab + FREQ), P(None, slab + FREQ), P())
    return jax.shard_map(local, mesh=parts, in_specs=in_specs, out_specs=out_specs, check_vma=False)
```

```python
import jax
import jax.numpy as jnp
from jax import lax
from jax.experimental import pallas as pl
from jax.experimental.pallas import tpu as pltpu
from jax.sharding import PartitionSpec as P

LANES = 128
PAIRS = 16
SLOTS = 16
EDGES = 12
GROUPS = 16
ROWS = 20
SLAB_ROWS = GROUPS * ROWS
PACK = 64
PER_STEP = 4
FREQ = ("y", "x_lo", "core")
PLANE = ("y", "x_lo", "core", "x_hi")
PARAMS_ALL = 3932160
FREQ_FIRST = 9
PLANE_FIRST = 19
Z_FIRST = 9
SPLITS = 3


def own_divisor(cells):
    owner = lax.axis_index(("x_hi", "z")) * GROUPS + lax.axis_index(FREQ)
    offset = cells - owner * (ROWS * LANES)
    inside = (offset >= 0) & (offset < ROWS * LANES)
    row = jnp.where(inside, offset >> 7, -1)
    lane = offset & (LANES - 1)
    place = lax.broadcasted_iota(jnp.int32, (PACK, LANES), 0)
    place = jnp.where(place < 2 * ROWS, jnp.where(place < ROWS, place, place - ROWS), place - 2 * ROWS)
    column = lax.broadcasted_iota(jnp.int32, (LANES, LANES), 0)
    row_hot, lane_hot = [], []
    for q in range(8):
        row_hot.append((row[q : q + 1, :] == place).astype(jnp.float32).astype(jnp.bfloat16))
        lane_hot.append((lane[q : q + 1, :] == column).astype(jnp.float32).astype(jnp.bfloat16))
    return 1.0 + 4.0 * lax.dot_general(
        jnp.concatenate(row_hot, axis=1),
        jnp.concatenate(lane_hot, axis=1),
        (((1,), (1,)), ((), ())),
        preferred_element_type=jnp.float32,
    )


def sens_kernel(
    ids,
    mass_in,
    weights_in,
    cells_in,
    fwd,
    adj,
    size,
    out,
    divisor,
    mass,
    weights,
    cells,
    e_buf,
    l_buf,
    scale_buf,
    mixed,
    e_sem,
    l_sem,
    small_sem,
):
    rows = PER_STEP * ROWS
    steps = GROUPS // PER_STEP
    small = [
        pltpu.make_async_copy(cells_in, cells, small_sem.at[3]),
        pltpu.make_async_copy(mass_in, mass, small_sem.at[0]),
        pltpu.make_async_copy(weights_in, weights, small_sem.at[1]),
        pltpu.make_async_copy(size, scale_buf, small_sem.at[2]),
    ]

    def copies(i):
        span = pl.ds(pl.multiple_of(i * 2 * rows, 2 * rows), 2 * rows)
        return (
            pltpu.make_async_copy(fwd.at[:, span, :], e_buf.at[:, span, :], e_sem.at[i]),
            pltpu.make_async_copy(adj.at[:, span, :], l_buf.at[:, span, :], l_sem.at[i]),
        )

    for copy in small:
        copy.start()
    for i in range(steps):
        for copy in copies(i):
            copy.start()
    small[0].wait()
    divisor[...] = own_divisor(cells[...])
    for copy in small[1:]:
        copy.wait()
    weight = weights[ids[0]]

    @pl.loop(0, steps)
    def _(i):
        for copy in copies(i):
            copy.wait()
        scale = scale_buf[pl.ds(pl.multiple_of(i * rows, 8), rows), :] * weight
        for k in range(3):
            factor = [[jnp.full((16, LANES), mass[k, a, b]) for b in range(4)] for a in range(4)]
            for first in range(0, 2 * rows, 16):
                span = pl.ds(pl.multiple_of(i * 2 * rows + first, 16), 16)
                e = [e_buf[4 * k + b, span, :].astype(jnp.float32) for b in range(4)]
                total = None
                for a in range(4):
                    coupled = factor[a][0] * e[0]
                    for b in range(1, 4):
                        coupled = coupled + factor[a][b] * e[b]
                    term = l_buf[4 * k + a, span, :].astype(jnp.float32) * coupled
                    total = term if total is None else total + term
                mixed[k, first : first + 16, :] = total
        for k in range(3):
            sens = mixed[k, pl.ds(0, rows, stride=2), :] - mixed[k, pl.ds(1, rows, stride=2), :]
            sens = sens * scale
            for owner in range(PER_STEP):
                out[(i ^ FREQ_FIRST // PER_STEP) * PER_STEP + (owner ^ FREQ_FIRST % PER_STEP), k * ROWS : (k + 1) * ROWS, :] = sens[owner * ROWS : (owner + 1) * ROWS, :]


def sens_to_owners(fwd, adj, mass, size, weights, ids, cells):
    smem = pl.BlockSpec(memory_space=pltpu.SMEM)
    hbm = pl.BlockSpec(memory_space=pltpu.HBM)
    rows = PER_STEP * ROWS
    steps = GROUPS // PER_STEP
    return pl.pallas_call(
        sens_kernel,
        out_shape=(
            jax.ShapeDtypeStruct((GROUPS, PACK, LANES), jnp.float32),
            jax.ShapeDtypeStruct((PACK, LANES), jnp.float32),
        ),
        in_specs=[smem, hbm, hbm, hbm, hbm, hbm, hbm],
        out_specs=(pl.BlockSpec(memory_space=pltpu.VMEM),) * 2,
        scratch_shapes=[
            pltpu.SMEM(mass.shape, mass.dtype),
            pltpu.SMEM(weights.shape, weights.dtype),
            pltpu.VMEM(cells.shape, cells.dtype),
            pltpu.VMEM(fwd.shape, fwd.dtype),
            pltpu.VMEM(adj.shape, adj.dtype),
            pltpu.VMEM(size.shape, size.dtype),
            pltpu.VMEM((3, 2 * rows, LANES), jnp.float32),
            pltpu.SemaphoreType.DMA((steps,)),
            pltpu.SemaphoreType.DMA((steps,)),
            pltpu.SemaphoreType.DMA((4,)),
        ],
        compiler_params=pltpu.CompilerParams(vmem_limit_bytes=12 << 20),
        name="sens",
    )(ids, *[pltpu.with_memory_space_constraint(each, pltpu.HBM) for each in (mass, weights, cells, fwd, adj, size)])


def split(values):
    parts = []
    for _ in range(SPLITS):
        parts.append(values.astype(jnp.bfloat16))
        values = values - parts[-1].astype(jnp.float32)
    return parts


def products_kernel(
    divisor, sens, steps, grads, gradient_out, precond, out, gradient, total_rows, damped_rows, gradient_sem
):
    total = sens[0:PACK, :]
    for f in range(1, SLOTS):
        total = total + sens[f * PACK : (f + 1) * PACK, :]
    total_rows[...] = total
    for r in range(ROWS):
        gradient[:, r * LANES : (r + 1) * LANES] = total_rows[pl.ds(r, 3, stride=ROWS), :]
    gradient_copy = pltpu.make_async_copy(gradient, gradient_out, gradient_sem)
    gradient_copy.start()
    damped_rows[...] = total / divisor[...]
    products = jnp.zeros((144, 144), jnp.float32)
    for k in range(3):
        slots, damped = [], []
        for r in range(ROWS):
            slots.append(sens[pl.ds(k * ROWS + r, SLOTS, stride=PACK), :])
            damped.append(jnp.broadcast_to(damped_rows[k * ROWS + r : k * ROWS + r + 1, :], (16, LANES)))
        pairs = split(jnp.concatenate([steps[k], grads[k]], axis=0))
        slots = split(jnp.concatenate(slots, axis=1))
        damped = split(jnp.concatenate(damped, axis=1))
        products = products + lax.dot_general(
            jnp.concatenate([*pairs, *slots], axis=0),
            jnp.concatenate([*pairs, *damped], axis=0),
            (((1,), (1,)), ((), ())),
            preferred_element_type=jnp.float32,
        )
    products = sum(
        products[:, 32 * b : 32 * b + 32] for b in reversed(range(SPLITS))
    ), sum(products[:, 32 * SPLITS + 16 * b : 32 * SPLITS + 16 * b + 16] for b in reversed(range(SPLITS)))
    products = jnp.concatenate(products, axis=1)
    products = jnp.concatenate(
        [
            sum(products[32 * a : 32 * a + 32] for a in reversed(range(SPLITS))),
            sum(products[32 * SPLITS + 16 * a : 32 * SPLITS + 16 * a + 16] for a in reversed(range(SPLITS))),
        ],
        axis=0,
    )
    s, y, f = products[:16], products[16:32], products[32:]
    row = lax.broadcasted_iota(jnp.int32, (16, 16), 0)
    lane = lax.broadcasted_iota(jnp.int32, (16, 16), 1)
    grad_gram = y[:, 16:32]
    block = jnp.concatenate(
        [
            jnp.where(row <= lane, s[:, 16:32], grad_gram),
            jnp.sum(jnp.where(row == lane, grad_gram, 0.0), axis=1, keepdims=True),
            f[:, 0:32],
            s[:, 32:33],
            y[:, 32:33],
            f[:, 32:33],
            jnp.zeros((16, 12), jnp.float32),
        ],
        axis=1,
    )
    block = jnp.concatenate([block[:8], block[8:]], axis=1)
    for i in range(out.shape[0]):
        out[i] = block
    for r in range(ROWS):
        precond[:, r * LANES : (r + 1) * LANES] = damped_rows[pl.ds(r, 3, stride=ROWS), :]
    gradient_copy.wait()


def inner_products(divisor, sens, steps, grads, copies):
    vmem = pl.BlockSpec(memory_space=pltpu.VMEM)
    own = jax.ShapeDtypeStruct((3, ROWS * LANES), jnp.float32)
    return pl.pallas_call(
        products_kernel,
        out_shape=(own, own, jax.ShapeDtypeStruct((copies, 8, LANES), jnp.float32)),
        in_specs=[vmem] * 4,
        out_specs=(pl.BlockSpec(memory_space=pltpu.HBM), vmem, vmem),
        scratch_shapes=[
            pltpu.VMEM(own.shape, own.dtype),
            pltpu.VMEM((PACK, LANES), jnp.float32),
            pltpu.VMEM((PACK, LANES), jnp.float32),
            pltpu.SemaphoreType.DMA(()),
        ],
        compiler_params=pltpu.CompilerParams(vmem_limit_bytes=12 << 20),
        name="products",
    )(divisor, sens, steps, grads)


def resend_kernel(parts, out):
    total = jnp.sum(parts[...], axis=0)
    for i in range(out.shape[0]):
        out[i] = total


def resend(parts, copies):
    vmem = pl.BlockSpec(memory_space=pltpu.VMEM)
    return pl.pallas_call(
        resend_kernel,
        out_shape=jax.ShapeDtypeStruct((copies, 8, LANES), jnp.float32),
        in_specs=[vmem],
        out_specs=vmem,
        compiler_params=pltpu.CompilerParams(vmem_limit_bytes=4 << 20),
        name="resend",
    )(parts)


def direction_kernel(parts, steps, grads, precond, direction, predicted):
    halves = jnp.sum(parts[...], axis=0)
    block = jnp.concatenate([halves[:, :64], halves[:, 64:]], axis=0)
    turned = jnp.concatenate([block, jnp.zeros((16, 64), jnp.float32)], axis=1)
    turned = jnp.concatenate([turned, jnp.zeros((LANES - 16, LANES), jnp.float32)], axis=0).T[:16]
    row = lax.broadcasted_iota(jnp.int32, (16, LANES), 0)
    lane = lax.broadcasted_iota(jnp.int32, (16, LANES), 1)

    def column(i, of=block):
        return jnp.broadcast_to(of[:, i : i + 1], (16, LANES))

    def place(i, value, into):
        return jnp.where(row == i, jnp.broadcast_to(value, (16, LANES)), into)

    diagonal = jnp.where(row[:, :64] == lane[:, :64], block, 0.0)
    diagonal = jnp.broadcast_to(jnp.sum(diagonal, axis=1, keepdims=True), (16, LANES))
    grad_diagonal = column(16)
    gamma = jnp.broadcast_to(diagonal[15:16, :] / grad_diagonal[15:16, :], (16, LANES))
    rest = column(49)
    first = jnp.zeros((16, LANES), jnp.float32)
    along = jnp.zeros((16, LANES), jnp.float32)
    slots_first = jnp.zeros((16, LANES), jnp.float32)
    for m in range(15, -1, -1):
        value = rest[m : m + 1, :] / diagonal[m : m + 1, :]
        upper = column(m)
        rest = rest - upper * value
        grad_column = jnp.where(row > m, upper, jnp.where(row < m, column(m, turned), grad_diagonal))
        along = along + grad_column * value
        slots_first = slots_first + column(33 + m) * value
        first = place(m, value, first)
    rest = diagonal * first + gamma * along - gamma * column(50)
    second = jnp.zeros((16, LANES), jnp.float32)
    slots_second = jnp.zeros((16, LANES), jnp.float32)
    for m in range(16):
        value = rest[m : m + 1, :] / diagonal[m : m + 1, :]
        rest = rest - column(m, turned) * value
        slots_second = slots_second + column(17 + m) * value
        second = place(m, value, second)
    change = -(gamma * column(51) + slots_second - gamma * slots_first) / PARAMS_ALL
    predicted[...] = jnp.sum(jnp.where(row == (lane ^ FREQ_FIRST), change, 0.0), axis=0)[:SLOTS]
    scaled = gamma * first
    for k in range(3):
        for r in range(ROWS):
            span = slice(r * LANES, (r + 1) * LANES)
            terms = second * steps[k, :, span] - scaled * grads[k, :, span]
            total = jnp.sum(terms, axis=0, keepdims=True)
            direction[k : k + 1, span] = -(gamma[0:1, :] * precond[k : k + 1, span] + total)


def directions(parts, steps, grads, precond):
    vmem = pl.BlockSpec(memory_space=pltpu.VMEM)
    own = jax.ShapeDtypeStruct((3, ROWS * LANES), jnp.float32)
    return pl.pallas_call(
        direction_kernel,
        out_shape=(own, jax.ShapeDtypeStruct((SLOTS,), jnp.float32)),
        in_specs=[vmem] * 4,
        out_specs=(vmem, vmem),
        compiler_params=pltpu.CompilerParams(vmem_limit_bytes=8 << 20),
        name="direction",
    )(parts, steps, grads, precond)


def field_rows(field):
    split = field.reshape(2, EDGES, SLAB_ROWS, LANES)
    return split.transpose(1, 2, 0, 3).reshape(EDGES, 2 * SLAB_ROWS, LANES)


def listed(count, first):
    return [[(i + first) % count for i in range(count)]]


def farthest_first(count, first):
    return [[first] + [(first + side * far) % count for far in range(count // 2, 0, -1) for side in (1, -1)][1:]]


def local(
    forward_field,
    adjoint_field,
    mass_block,
    cell_size,
    freq_weight,
    freq_ids,
    receiver_cells,
    step_pairs,
    grad_pairs,
):
    steps = step_pairs.transpose(1, 0, 2)
    grads = grad_pairs.transpose(1, 0, 2)
    packed, divisor = sens_to_owners(
        field_rows(forward_field),
        field_rows(adjoint_field),
        mass_block,
        cell_size.reshape(SLAB_ROWS, LANES),
        freq_weight,
        freq_ids,
        receiver_cells.reshape(8, LANES),
    )
    arrived = lax.all_to_all(packed, FREQ, 0, 0, tiled=True, axis_index_groups=[[i ^ FREQ_FIRST for i in range(16)]])
    gradient, precond, block = inner_products(
        divisor,
        arrived.reshape(SLOTS * PACK, LANES),
        steps,
        grads,
        lax.axis_size(PLANE),
    )
    parts = lax.all_to_all(block, PLANE, 0, 0, tiled=True, axis_index_groups=listed(32, PLANE_FIRST))
    parts = lax.all_to_all(resend(parts, lax.axis_size("z")), "z", 0, 0, tiled=True, axis_index_groups=farthest_first(16, Z_FIRST))
    direction, predicted = directions(parts, steps, grads, precond)
    return (gradient, direction, predicted)


def solution(mesh):
    axes = ("y", "x_lo", "core", "x_hi", "z")
    parts = jax.sharding.Mesh(mesh.devices.reshape(4, 2, 2, 2, 16), axes)
    slab = ("x_hi", "z")
    owned = P(None, None, slab + FREQ)
    in_specs = (
        P(FREQ, None, None, slab),
        P(FREQ, None, None, slab),
        P(),
        P(slab),
        P(),
        P(FREQ),
        P(),
        owned,
        owned,
    )
    out_specs = (P(None, slab + FREQ), P(None, slab + FREQ), P())
    return jax.shard_map(local, mesh=parts, in_specs=in_specs, out_specs=out_specs, check_vma=False)
```
